32 devices in a mesh: seq: 8 (over z, y), mp: 4 (over x, core).
Axes of the slice: x: 2, y: 2, z: 4, core: 2. Of those that a mesh axis runs over, the one named last changes fastest.
Arguments:
- scored_token_targets: int32 [2048], P('seq'), may hold values from 0 to 15999
- valid: int32 [2048], P('seq'), may hold values 0 or 1
- lengths: int32 [48], replicated, may hold values from 1 to 256, 2048 in all
- owners: int32 [48], replicated, may hold values from 0 to 7
- holders: int32 [48], replicated, may hold values from -1 to 7, as said below
- mixer_input_x: bfloat16 [2, 2048, 3584], P(None, 'seq', 'mp'), may hold values from -6 to 6
- mixer_gate_input: bfloat16 [2, 2048, 3584], P(None, 'seq', 'mp'), may hold values from -6 to 6
- input_projection_b: bfloat16 [2, 2048, 64], P(None, 'seq'), may hold values from -2.390625 to 2.390625
- output_projection_c: bfloat16 [2, 2048, 64], P(None, 'seq'), may hold values from -2.390625 to 2.390625
- token_step_sizes: float32 [2, 2048, 56], P(None, 'seq', 'mp'), may hold values from 0.01 to 0.3
- head_decay_rate: float32 [2, 56], P(None, 'mp'), may hold values from 0.0002 to 1
- head_skip_scale: float32 [2, 56], P(None, 'mp'), may hold values from 0.5 to 1.5
- prompt_held_states: bfloat16 [2, 8, 56, 64, 64], P(None, 'seq', 'mp'), may hold values from -6 to 6
- shared_output_weight: bfloat16 [3584, 3584], P('mp'), may hold values from -0.09375 to 0.09375
- adapter_down_weight: bfloat16 [3584, 128], P('mp'), may hold values from -0.09375 to 0.09375
- adapter_up_weight: bfloat16 [128, 3584], replicated, may hold values from -0.5 to 0.5
- residual: bfloat16 [2048, 2, 3584], P('seq'), may hold values from -16 to 16
- final_norm_scale: float32 [3584], replicated, may hold values from 0.5 to 1.5
- vocab_head_weight: bfloat16 [3584, 16000], P('seq', 'mp'), may hold values from -8 to 8
Outputs:
- owner_sums: float32 [8, 48], P('seq')
- token_delta: float32 [2048], P('seq')
The draws below stay inside these ranges and needn't reach their ends.
Inputs may be any that keep to these rules, and one draw needn't show every extreme that they name: `holders`: exactly 24 rollouts continue a prompt state; the others start from zeros.
All inputs are finite; a program needn't handle non-finite values. No bound on the sum of `valid` on one device may be relied on, other than what follows from the above.
Results may differ from the reference program's by a relative error of at most 0.035.
Values may be sent and summed in bfloat16 or wider, within the bound.
No kernel may reach another device: no remote copies, remote signals or barrier semaphores. Data moves between devices by JAX's collectives and lax.ppermute only.
A program may use at most 128 MiB of HBM per device.

```python
import math
import jax
import jax.numpy as jnp
import numpy as np
from jax import lax

MODEL_WIDTH = 3584
HEADS = 56
HEAD = 64
STATE = 64
VOCAB = 16000
ADAPTER_RANK = 128
ROLLOUTS = 48
MIXER_WIDTH = 3584
TOKENS = 2048
LEN_MOST = 256
N_SEQ = 8
N_MP = 4


def draw_holders(key, part):
    order_key = jax.random.fold_in(key, 11)
    source_key = jax.random.fold_in(key, 12)
    order = jax.random.permutation(order_key, ROLLOUTS)
    source = jax.random.randint(source_key, (ROLLOUTS,), 0, N_SEQ)
    source = jnp.where(order == 0, N_SEQ - 1, source)
    return jnp.where(order < ROLLOUTS // 2, source, -1).astype(jnp.int32)


def drawn_parts(key):
    base_key = jax.random.fold_in(key, 31)
    signs = jax.random.randint(jax.random.fold_in(base_key, 1), (4, MODEL_WIDTH), 0, 2).astype(jnp.float32) * 2.0 - 1.0
    rows_picked = jax.random.randint(jax.random.fold_in(base_key, 2), (16,), 0, TOKENS)
    cols_picked = jax.random.permutation(jax.random.fold_in(base_key, 3), VOCAB)[:8]
    return (signs, rows_picked, cols_picked)


def draw_residual(key, part):
    signs, rows_picked, cols_picked = drawn_parts(key)
    noise_key = jax.random.fold_in(key, 41)
    noise = jnp.clip(jax.random.normal(noise_key, (TOKENS, 2, MODEL_WIDTH), jnp.float32), -6.0, 6.0)
    row_dir = jnp.full((TOKENS,), -1, jnp.int32).at[rows_picked].set(jnp.arange(16, dtype=jnp.int32) % 4)
    picked = jnp.take(signs, jnp.maximum(row_dir, 0), axis=0)
    return jnp.where((row_dir >= 0)[:, None, None], noise + 8.0 * picked[:, None, :], noise).astype(jnp.bfloat16)


def draw_vocab_head_weight(key, part):
    signs, rows_picked, cols_picked = drawn_parts(key)
    noise_key = jax.random.fold_in(key, 42)
    spread = (MODEL_WIDTH // 9) ** (-0.5)
    noise = jnp.clip(jax.random.normal(noise_key, (MODEL_WIDTH, VOCAB), jnp.float32), -6.0, 6.0) * spread
    strengths = jnp.array([120.0, 180.0, 260.0, 340.0], jnp.float32)
    index = jnp.arange(8, dtype=jnp.int32)
    which = index // 2
    power = strengths[which]
    factor = power / MODEL_WIDTH * jnp.where(index % 2 == 1, 1.0 - 2.0 / power, 1.0)
    columns = jnp.transpose(jnp.take(signs, which, axis=0)) * factor[None, :]
    return noise.at[:, cols_picked].set(columns).astype(jnp.bfloat16)


def plant(values, own_key, low, largest):
    longest = values.shape.index(max(values.shape))
    spots = []
    for shift in (0, 1):
        where = [jax.random.randint(jax.random.fold_in(own_key, axis), (), 0, length) for axis, length in enumerate(values.shape)]
        where[longest] = (where[longest] + shift) % values.shape[longest]
        spots.append(tuple(where))
    return values.at[spots[0]].set(low).at[spots[1]].set(largest)


def steps_of(key, dims, cuts, least, high):
    gain, own = 1.0, jax.random.fold_in(key, 6)
    for dim, blocks in cuts:
        steps = jnp.exp(jax.random.uniform(jax.random.fold_in(own, dim), (blocks,), jnp.float32, least / len(cuts), high / len(cuts)))
        gain = gain * jnp.repeat(steps, dims[dim] // blocks).reshape([-1 if axis == dim else 1 for axis in range(len(dims))])
    return gain


def cumulative_ranks(number_of, lean):
    weights = [(1 << 20) // math.isqrt(rank ** lean) + 1 for rank in range(1, number_of + 1)]
    scale = 1 + sum(weights) // (1 << 30)
    return np.cumsum(np.array([max(1, weight // scale) for weight in weights]))


def ranked(stream_key, dims, amount, slope):
    grid = cumulative_ranks(amount, slope)
    lot = jax.random.randint(jax.random.fold_in(stream_key, 1), dims, 0, int(grid[amount - 1]))
    standing = jnp.searchsorted(jnp.asarray(grid, jnp.int32), lot, side="right")
    return jax.random.permutation(jax.random.fold_in(stream_key, 2), amount)[standing].astype(jnp.int32)


def profile(amount, total, most, slope):
    weights = [(1 << 20) // math.isqrt(standing ** slope) + 1 for standing in range(2, amount + 1)]
    spare, given = total - most - (amount - 1), [1] * (amount - 1)
    while spare > 0:
        candidates = [i for i in range(amount - 1) if given[i] < most]
        mass, remaining = sum([weights[i] for i in candidates]), spare
        for i in candidates:
            extra = min(most - given[i], max(1, remaining * weights[i] // mass), spare)
            given[i] = given[i] + extra
            spare = spare - extra
    return np.array([most] + given)


def ragged_sizes(stream_key, number_of, total, limit, slope):
    if number_of == 2:
        one = jax.random.randint(stream_key, (), max(1, total - limit), min(limit, total - 1) + 1)
        return jnp.stack([one, total - one])
    sizes = jnp.asarray(profile(number_of, total, limit, slope), jnp.int32)
    couples = (number_of - 1) // 2
    source_of, taker = sizes[1:1 + 2 * couples:2], sizes[2:2 + 2 * couples:2]
    margin = jnp.minimum(source_of - 1, limit - taker)
    shifted = jax.random.randint(jax.random.fold_in(stream_key, 1), (couples,), 0, 1 << 20) % (margin + 1)
    sizes = sizes.at[1:1 + 2 * couples:2].set(source_of - shifted).at[2:2 + 2 * couples:2].set(taker + shifted)
    return sizes[jax.random.permutation(jax.random.fold_in(stream_key, 2), number_of)]


def scatter_about(key, shape, scale, most, split=(), held_as=jnp.bfloat16):
    gain = steps_of(key, shape, split, -0.22, 0.18) if split else 1.0
    values = jax.random.normal(key, shape, jnp.float32) * scale * gain
    return jnp.minimum(jnp.maximum(values, -most), most).astype(held_as)


def setup_inputs(seed: int = 0) -> dict:
    seeds = jax.random.split(jax.random.key(seed), 20)
    return {
        "scored_token_targets": plant(ranked(seeds[0], (TOKENS,), VOCAB, 2), jax.random.fold_in(seeds[0], 3), 0, VOCAB - 1).astype(jnp.int32),
        "valid": plant((jax.random.randint(seeds[1], (TOKENS,), 0, 8) < 7).astype(jnp.int32), jax.random.fold_in(seeds[1], 1), 0, 1),
        "lengths": ragged_sizes(seeds[2], ROLLOUTS, TOKENS, LEN_MOST, 2).astype(jnp.int32),
        "owners": plant(jax.random.randint(seeds[3], (ROLLOUTS,), 0, N_SEQ), jax.random.fold_in(seeds[3], 1), 0, N_SEQ - 1).astype(jnp.int32),
        "holders": draw_holders(jax.random.fold_in(seeds[19], 71), 0),
        "mixer_input_x": scatter_about(seeds[5], (2, TOKENS, MIXER_WIDTH), 1.0, 6.0, ((1, 8), (2, 4))),
        "mixer_gate_input": scatter_about(seeds[6], (2, TOKENS, MIXER_WIDTH), 1.0, 6.0, ((1, 8), (2, 4))),
        "input_projection_b": scatter_about(seeds[7], (2, TOKENS, STATE), 0.4, 2.390625, ((1, 8),)),
        "output_projection_c": scatter_about(seeds[8], (2, TOKENS, STATE), 0.4, 2.390625, ((1, 8),)),
        "token_step_sizes": jnp.clip(jnp.exp(math.log(0.3) - 3.4011974 * jax.random.uniform(seeds[9], (2, TOKENS, HEADS), jnp.float32) ** steps_of(seeds[9], (2, TOKENS, HEADS), ((1, 8), (2, 4)), -0.2, 0.2)), 0.01, 0.3),
        "head_decay_rate": jnp.clip(jnp.exp(math.log(1.0) - 8.517193 * jax.random.uniform(seeds[10], (2, HEADS), jnp.float32) ** steps_of(seeds[10], (2, HEADS), ((1, 4),), -0.2, 0.2)), 0.0002, 1.0),
        "head_skip_scale": jnp.clip(0.5 + 1.0 * jax.random.uniform(seeds[11], (2, HEADS), jnp.float32) ** steps_of(seeds[11], (2, HEADS), ((1, 4),), -0.2, 0.2), 0.5, 1.5),
        "prompt_held_states": scatter_about(seeds[12], (2, N_SEQ, HEADS, HEAD, STATE), 1.0, 6.0, ((1, 8), (2, 4))),
        "shared_output_weight": scatter_about(seeds[13], (MIXER_WIDTH, MODEL_WIDTH), MIXER_WIDTH ** -0.5, 0.09375, ((0, 4),)),
        "adapter_down_weight": scatter_about(seeds[14], (MIXER_WIDTH, ADAPTER_RANK), MIXER_WIDTH ** -0.5, 0.09375, ((0, 4),)),
        "adapter_up_weight": scatter_about(seeds[15], (ADAPTER_RANK, MODEL_WIDTH), ADAPTER_RANK ** -0.5, 0.5),
        "residual": draw_residual(jax.random.fold_in(seeds[19], 71), 0),
        "final_norm_scale": jnp.clip(1.0 + 0.1 * jax.random.normal(seeds[17], (MODEL_WIDTH,), jnp.float32), 0.5, 1.5),
        "vocab_head_weight": draw_vocab_head_weight(jax.random.fold_in(seeds[19], 71), 0),
    }


highest = lax.Precision.HIGHEST

def root_norm(hidden, final_norm_scale):
    mean_sq = lax.optimization_barrier(jnp.mean(hidden * hidden, axis=-1, keepdims=True))
    return (hidden * lax.rsqrt(mean_sq + 1e-05) * final_norm_scale).astype(jnp.bfloat16)

def reference(scored_token_targets, valid, lengths, owners, holders, mixer_input_x, mixer_gate_input, input_projection_b, output_projection_c, token_step_sizes, head_decay_rate, head_skip_scale, prompt_held_states, shared_output_weight, adapter_down_weight, adapter_up_weight, residual, final_norm_scale, vocab_head_weight):
    position = jnp.arange(TOKENS, dtype=jnp.int32)
    starts = (jnp.cumsum(lengths) - lengths).astype(jnp.int32)
    rollout = (lax.optimization_barrier(jnp.sum((starts[None, :] <= position[:, None]).astype(jnp.int32), axis=1)) - 1).astype(jnp.int32)
    is_start = jnp.take(starts, rollout) == position
    holder_tok = jnp.take(holders, rollout).astype(jnp.int32)
    neg_rates = -head_decay_rate.astype(jnp.float32)
    x_values = jnp.transpose(mixer_input_x.astype(jnp.float32).reshape(2, TOKENS, HEADS, HEAD), (1, 0, 2, 3))
    b_values = jnp.transpose(input_projection_b.astype(jnp.float32), (1, 0, 2))
    c_values = jnp.transpose(output_projection_c.astype(jnp.float32), (1, 0, 2))
    dt_values = jnp.transpose(token_step_sizes.astype(jnp.float32), (1, 0, 2))

    def advance(state, inputs):
        x_now, b_now, c_now, dt_now, start_now, hold_now = inputs
        prompt = lax.dynamic_index_in_dim(prompt_held_states, jnp.maximum(hold_now, 0), axis=1, keepdims=False).astype(jnp.float32)
        prompt = jnp.where(hold_now >= 0, prompt, jnp.zeros_like(prompt))
        state = jnp.where(start_now, prompt, state)
        factor = jnp.exp(dt_now * neg_rates)
        state = factor[:, :, None, None] * state + (dt_now[:, :, None] * x_now)[:, :, :, None] * b_now[:, None, None, :]
        y_now = jnp.einsum('mhpn,mn->mhp', state, c_now, precision=highest)
        return (state, y_now)
    state_zero = jnp.zeros((2, HEADS, HEAD, STATE), jnp.float32)
    final_state, y_values = lax.scan(advance, state_zero, (x_values, b_values, c_values, dt_values, is_start, holder_tok))
    y_values = y_values + head_skip_scale.astype(jnp.float32)[None, :, :, None] * x_values
    y_values = y_values.reshape(TOKENS, 2, MIXER_WIDTH)
    gate_values = jnp.transpose(mixer_gate_input.astype(jnp.float32), (1, 0, 2))
    gated_output = (y_values * jax.nn.silu(gate_values)).astype(jnp.bfloat16)
    layer_width = MIXER_WIDTH // N_MP

    def add_block(holder_index, running):
        part_rows = lax.dynamic_slice_in_dim(gated_output, holder_index * layer_width, layer_width, 2)
        weight_rows = lax.dynamic_slice_in_dim(shared_output_weight, holder_index * layer_width, layer_width, 0)
        adapter_down_rows = lax.dynamic_slice_in_dim(adapter_down_weight, holder_index * layer_width, layer_width, 0)
        base_output = jnp.einsum('tmi,id->tmd', part_rows.astype(jnp.float32), weight_rows.astype(jnp.float32))
        low_rank_rows = jnp.dot(part_rows[:, 0], adapter_down_rows, preferred_element_type=jnp.float32).astype(jnp.bfloat16)
        adapter_output = jnp.dot(low_rank_rows, adapter_up_weight, preferred_element_type=jnp.float32)
        adapter_term_rows = jnp.stack([base_output[:, 0] + adapter_output, base_output[:, 1]], axis=1).astype(jnp.bfloat16)
        adapter_term_rows = lax.optimization_barrier(adapter_term_rows)
        return running + adapter_term_rows.astype(jnp.float32)
    mixed = lax.fori_loop(0, N_MP, add_block, jnp.zeros((TOKENS, 2, MODEL_WIDTH), jnp.float32))
    normed = root_norm(residual.astype(jnp.float32) + mixed, final_norm_scale)
    logprobs = []
    for model_index in range(2):
        logits = jnp.dot(normed[:, model_index], vocab_head_weight, preferred_element_type=jnp.float32)
        vocab_top = lax.optimization_barrier(jnp.max(logits, axis=1))
        vocab_total = lax.optimization_barrier(jnp.sum(jnp.exp(logits - vocab_top[:, None]), axis=1))
        target_logit = jnp.take_along_axis(logits, scored_token_targets[:, None].astype(jnp.int32), axis=1)[:, 0]
        logprobs.append(target_logit - vocab_top - jnp.log(vocab_total))
    token_delta = (logprobs[0] - logprobs[1]) * valid.astype(jnp.float32)
    member_table = (rollout[:, None] == jnp.arange(ROLLOUTS, dtype=jnp.int32)[None, :]).astype(jnp.float32)
    roll_sums = jnp.dot(token_delta, member_table, precision=highest) / lengths.astype(jnp.float32)
    owner_table = (owners[None, :] == jnp.arange(N_SEQ, dtype=jnp.int32)[:, None]).astype(jnp.float32)
    owner_sums = owner_table * roll_sums[None, :]
    return (owner_sums, token_delta)
```

```python
import itertools

import jax
import jax.numpy as jnp
from jax import lax
from jax.sharding import PartitionSpec as P

highest = lax.Precision.HIGHEST
CHAIN = 4
SIDE = 2


def place_of(i):
    return (i // SIDE) % CHAIN


def turned(i, by):
    return i + ((place_of(i) + by) % CHAIN - place_of(i)) * SIDE


def partner(i, side, block, count):
    return ((i ^ side) + block * CHAIN * SIDE) % count


def turn(x, by):
    count = lax.axis_size("seq")
    return lax.ppermute(x, "seq", [(i, turned(i, by)) for i in range(count)])


def to_partner(x, side, block):
    count = lax.axis_size("seq")
    return lax.ppermute(x, "seq", [(i, partner(i, side, block, count)) for i in range(count)])


def along_chain(x):
    count = lax.axis_size("seq")
    place = place_of(lax.axis_index("seq"))
    up, down, ups, downs = x, x, [], []
    for step in range(1, CHAIN):
        up = lax.ppermute(
            up, "seq", [(i, i + SIDE) for i in range(count) if step - 1 <= place_of(i) < CHAIN - 1]
        )
        down = lax.ppermute(
            down, "seq", [(i, i - SIDE) for i in range(count) if 0 < place_of(i) <= CHAIN - step]
        )
        ups.append(up)
        downs.append(down)
    return [x] + [
        jnp.where(place >= k, ups[k - 1], downs[CHAIN - k - 1]) for k in range(1, CHAIN)
    ]


def other_core(x):
    count = lax.axis_size("mp")
    return lax.ppermute(x, "mp", [(i, i ^ 1) for i in range(count)])


def along_x(x, by):
    count = lax.axis_size("mp")
    return lax.ppermute(x, "mp", [(i, (i + 2 * by) % count) for i in range(count)])


def shards(
    scored_token_targets,
    valid,
    lengths,
    owners,
    holders,
    mixer_input_x,
    mixer_gate_input,
    input_projection_b,
    output_projection_c,
    token_step_sizes,
    head_decay_rate,
    head_skip_scale,
    prompt_held_states,
    shared_output_weight,
    adapter_down_weight,
    adapter_up_weight,
    residual,
    final_norm_scale,
    vocab_head_weight,
):
    seq_count = lax.axis_size("seq")
    mp_count = lax.axis_size("mp")
    seq_index = lax.axis_index("seq")
    mp_index = lax.axis_index("mp")
    place = place_of(seq_index)
    core = mp_index % 2
    x_count = mp_count // 2
    x_index = mp_index // 2
    tok_rows = scored_token_targets.shape[0]
    models = mixer_input_x.shape[0]
    inner_local = mixer_input_x.shape[2]
    head_count = token_step_sizes.shape[2]
    head_dim = inner_local // head_count
    state_dim = input_projection_b.shape[2]
    roll_count = lengths.shape[0]
    width = residual.shape[2]
    blocks = seq_count // (CHAIN * SIDE)
    partners = list(itertools.product(range(SIDE), range(blocks)))

    head_rows, vocab_local = vocab_head_weight.shape
    part = -(-vocab_local // (CHAIN * 128)) * 128
    padded = jnp.pad(vocab_head_weight, ((0, 0), (0, CHAIN * part - vocab_local)))
    shares = [
        lax.dynamic_slice_in_dim(padded, (place + k) % CHAIN * part, part, 1)
        for k in range(CHAIN)
    ]
    came = [shares[0]] + [turn(shares[k], k) for k in range(1, CHAIN)]
    head_part = jnp.zeros((seq_count * head_rows, part), vocab_head_weight.dtype)
    for k in range(CHAIN):
        for side, block in partners:
            piece = came[k] if (side, block) == (0, 0) else to_partner(came[k], side, block)
            source = turned(partner(seq_index, side, blocks - block, seq_count), -k)
            head_part = lax.dynamic_update_slice_in_dim(head_part, piece, source * head_rows, 0)

    held = jnp.transpose(prompt_held_states[:, 0], (0, 3, 1, 2)).reshape(
        models, state_dim, inner_local
    )
    pieces, piece_holder = [], []
    for k, state in enumerate(along_chain(held)):
        for side, block in partners:
            pieces.append(state if (side, block) == (0, 0) else to_partner(state, side, block))
            piece_holder.append(turned(partner(seq_index, side, blocks - block, seq_count), -k))
    prompts = jnp.concatenate(pieces, axis=1)
    piece_holder = jnp.stack(piece_holder)

    first_row = seq_index * tok_rows
    offsets = jnp.arange(tok_rows, dtype=jnp.int32)
    position = first_row + offsets
    starts = jnp.cumsum(lengths) - lengths
    rollout = jnp.sum((starts[None, :] <= position[:, None]).astype(jnp.int32), axis=1) - 1
    member_table = rollout[:, None] == jnp.arange(roll_count, dtype=jnp.int32)[None, :]
    start_local = jnp.sum(jnp.where(member_table, starts[None, :], 0), axis=1) - first_row
    holder_tok = jnp.sum(jnp.where(member_table, holders[None, :], 0), axis=1)
    borrowed = (start_local >= 0) & (holder_tok >= 0)
    prompt_pick = (holder_tok[:, None] == piece_holder[None, :]) & borrowed[:, None]
    neg_rates = -head_decay_rate
    log_decay = jnp.cumsum(token_step_sizes * neg_rates[:, None, :], axis=1)
    before = jnp.take(log_decay, jnp.maximum(start_local - 1, 0), axis=1)
    before = jnp.where((start_local >= 1)[None, :, None], before, 0.0)
    x_values = mixer_input_x.astype(jnp.float32).reshape(models, tok_rows, head_count, head_dim)
    b_values = input_projection_b.astype(jnp.float32)
    c_values = output_projection_c.astype(jnp.float32)
    gram_matrix = jnp.einsum(
        "mtn,msn->mts", output_projection_c, input_projection_b, preferred_element_type=jnp.float32
    )
    causal = (rollout[:, None] == rollout[None, :]) & (offsets[None, :] <= offsets[:, None])
    log_gap = log_decay[:, :, None, :] - log_decay[:, None, :, :]
    mixing = jnp.where(
        causal[None, :, :, None], jnp.exp(jnp.where(causal[None, :, :, None], log_gap, 0.0)), 0.0
    )
    mixing = mixing * gram_matrix[..., None] * token_step_sizes[:, None, :, :]
    intra_out = jnp.einsum("mtsh,mshp->mthp", mixing, x_values, precision=highest)

    final_log = log_decay[:, tok_rows - 1, :]
    tail_mask = (rollout == rollout[tok_rows - 1]).astype(jnp.float32)
    end_weight = (
        jnp.exp(final_log[:, None, :] - log_decay) * token_step_sizes * tail_mask[None, :, None]
    )
    local_end = jnp.einsum("msh,mshp,msn->mnhp", end_weight, x_values, b_values, precision=highest)
    end_state = jnp.einsum(
        "j,mjnd->mnd",
        prompt_pick[tok_rows - 1].astype(jnp.bfloat16),
        prompts.reshape(models, seq_count, state_dim, inner_local),
        preferred_element_type=jnp.float32,
    ).reshape(models, state_dim, head_count, head_dim)
    local_end = (
        local_end
        + jnp.exp(final_log - before[:, tok_rows - 1, :])[:, None, :, None] * end_state
    ).reshape(models, state_dim, inner_local)
    carry_through = jnp.repeat(
        jnp.where(start_local[tok_rows - 1] < 0, jnp.exp(final_log), 0.0), head_dim, axis=1
    )
    hops = max(1, -(-(seq_count * tok_rows // 8) // tok_rows))
    next_one = [(i, i + 1) for i in range(seq_count - 1)]
    arriving = lax.ppermute(local_end, "seq", next_one)
    for _ in range(hops - 1):
        arriving = lax.ppermute(carry_through[:, None, :] * arriving + local_end, "seq", next_one)

    picked = (prompt_pick[None, :, :, None] * c_values[:, :, None, :]).astype(jnp.bfloat16)
    projected = jnp.einsum(
        "mtk,mkd->mtd",
        picked.reshape(models, tok_rows, seq_count * state_dim),
        prompts,
        preferred_element_type=jnp.float32,
    ).reshape(models, tok_rows, head_count, head_dim)
    inherited = (start_local < 0).astype(jnp.float32)
    carried = jnp.einsum(
        "mtn,mnd->mtd", c_values * inherited[None, :, None], arriving, precision=highest
    ).reshape(models, tok_rows, head_count, head_dim)
    entry_decay = jnp.exp(log_decay - before)
    output = (
        intra_out
        + entry_decay[..., None] * (projected + carried)
        + head_skip_scale[:, None, :, None] * x_values
    )
    output = output.reshape(models, tok_rows, inner_local)
    gated_output = (output * jax.nn.silu(mixer_gate_input.astype(jnp.float32))).astype(jnp.bfloat16)

    share_rows = tok_rows // mp_count
    base_output = jnp.einsum(
        "mti,id->mtd", gated_output, shared_output_weight, preferred_element_type=jnp.float32
    )
    low_rank_rows = jnp.dot(
        gated_output[0], adapter_down_weight, preferred_element_type=jnp.float32
    ).astype(jnp.bfloat16)
    adapter_output = jnp.dot(low_rank_rows, adapter_up_weight, preferred_element_type=jnp.float32)
    terms = jnp.stack([base_output[0] + adapter_output, base_output[1]]).astype(jnp.bfloat16)
    terms = terms.reshape(models, x_count, 2, share_rows, width)
    kept = lax.dynamic_index_in_dim(terms, core, 2, keepdims=False)
    sent = lax.dynamic_index_in_dim(terms, 1 - core, 2, keepdims=False)
    chip_sum = kept.astype(jnp.float32) + other_core(sent).astype(jnp.float32)
    mixed = lax.dynamic_index_in_dim(chip_sum, x_index, 1, keepdims=False)
    for by in range(1, x_count):
        away = lax.dynamic_index_in_dim(chip_sum, (x_index + by) % x_count, 1, keepdims=False)
        mixed = mixed + along_x(away.astype(jnp.bfloat16), by).astype(jnp.float32)
    own_rows = lax.dynamic_slice_in_dim(residual, mp_index * share_rows, share_rows, 0)
    hidden = jnp.transpose(own_rows, (1, 0, 2)).astype(jnp.float32) + mixed
    mean_sq = jnp.mean(hidden * hidden, axis=-1, keepdims=True)
    normed_own = (hidden * lax.rsqrt(mean_sq + 1e-05) * final_norm_scale).astype(jnp.bfloat16)
    normed_own = normed_own.reshape(models * share_rows, width)

    column = place * part + jnp.arange(part, dtype=jnp.int32)
    in_range = column < vocab_local
    word = mp_index * vocab_local + column
    gathered = None
    for k, rows in enumerate(along_chain(normed_own)):
        targets = scored_token_targets if k == 0 else turn(scored_token_targets, k)
        beside = [rows] + [along_x(rows, by) for by in range(1, x_count)]
        both = jnp.stack(beside)
        opposite = other_core(both)
        order_x = (x_index - jnp.arange(x_count, dtype=jnp.int32)) % x_count
        own_mp = order_x * 2 + core
        other_mp = order_x * 2 + 1 - core
        row_mp = jnp.concatenate([own_mp, other_mp])
        all_rows = jnp.concatenate([both, opposite])
        targets = targets.reshape(mp_count, share_rows)[row_mp]
        logits = jnp.einsum(
            "rk,kv->rv",
            all_rows.reshape(mp_count * models * share_rows, width),
            head_part,
            preferred_element_type=jnp.float32,
        ).reshape(mp_count, models, share_rows, part)
        logits = jnp.where(in_range, logits, -jnp.inf)
        hit = (targets[:, :, None] == word) & in_range
        target_logit = jnp.sum(jnp.where(hit[:, None], logits, 0.0), axis=3)
        top = jnp.max(logits, axis=3)
        total = jnp.sum(jnp.exp(logits - top[..., None]), axis=3)
        stats = jnp.stack([top, total, target_logit])
        stats = jnp.zeros_like(stats).at[:, row_mp].set(stats)
        stats = stats if k == 0 else turn(stats, -k)
        gathered = [stats] if k == 0 else gathered + [stats]

    def merged(stats):
        top = jnp.max(stats[:, 0], axis=0)
        total = jnp.sum(stats[:, 1] * jnp.exp(stats[:, 0] - top), axis=0)
        return jnp.stack([top, total, jnp.sum(stats[:, 2], axis=0)])

    chain_stats = merged(jnp.stack(gathered))
    top, total, target_logit = merged(lax.all_gather(chain_stats, "mp", axis=0))
    logprob = target_logit - top - jnp.log(total)
    token_delta = (logprob[:, 0] - logprob[:, 1]).reshape(tok_rows) * valid.astype(jnp.float32)
    roll_sums = jnp.dot(
        token_delta, member_table.astype(jnp.float32), precision=highest
    ) / lengths.astype(jnp.float32)
    owner_rows = (owners[None, :] == jnp.arange(seq_count, dtype=jnp.int32)[:, None]).astype(
        jnp.float32
    ) * roll_sums[None, :]
    owner_sums = lax.psum_scatter(owner_rows, "seq", scatter_dimension=0, tiled=True)
    return (owner_sums, token_delta)


def solution(mesh):
    placed = (
        P("seq"),
        P("seq"),
        P(),
        P(),
        P(),
        P(None, "seq", "mp"),
        P(None, "seq", "mp"),
        P(None, "seq", None),
        P(None, "seq", None),
        P(None, "seq", "mp"),
        P(None, "mp"),
        P(None, "mp"),
        P(None, "seq", "mp", None, None),
        P("mp", None),
        P("mp", None),
        P(),
        P("seq", None, None),
        P(),
        P("seq", "mp"),
    )
    return jax.shard_map(
        shards, mesh=mesh, in_specs=placed, out_specs=(P("seq", None), P("seq")), check_vma=False
    )
```

```python
import functools
import itertools

import jax
import jax.numpy as jnp
from jax import lax
from jax.experimental import pallas as pl
from jax.experimental.pallas import tpu as pltpu
from jax.sharding import PartitionSpec as P

highest = lax.Precision.HIGHEST
CHAIN = 4
SIDE = 2


def place_of(i):
    return (i // SIDE) % CHAIN


def turned(i, by):
    return i ^ (by * SIDE)


def partner(i, side, block, count):
    return ((i ^ side) + block * CHAIN * SIDE) % count


def turn(x, by):
    count = lax.axis_size("seq")
    return lax.ppermute(x, "seq", [(i, turned(i, by)) for i in range(count)])


def to_partner(x, side, block):
    count = lax.axis_size("seq")
    return lax.ppermute(x, "seq", [(i, partner(i, side, block, count)) for i in range(count)])


def chain_groups():
    count = lax.axis_size("seq")
    return [
        [first + k * SIDE for k in range(CHAIN)] for first in range(count) if place_of(first) == 0
    ]


def other_core(x):
    count = lax.axis_size("mp")
    return lax.ppermute(x, "mp", [(i, i ^ 1) for i in range(count)])


def along_x(x, by):
    count = lax.axis_size("mp")
    return lax.ppermute(x, "mp", [(i, (i + 2 * by) % count) for i in range(count)])


def tied(*values):
    return lax.optimization_barrier(values)


def dot(a, b, over=((1,), (0,))):
    return lax.dot_general(a, b, (over, ((), ())), preferred_element_type=jnp.float32)


def head_pairs(head_count, head_dim):
    return [
        (first, slice(first * head_dim, min(first + 2, head_count) * head_dim))
        for first in range(0, head_count, 2)
    ]


def pair_lanes(values, first, head_dim):
    if first + 1 == values.shape[1]:
        return jnp.broadcast_to(values[:, first : first + 1], (values.shape[0], head_dim))
    lane = lax.broadcasted_iota(jnp.int32, (values.shape[0], 2 * head_dim), 1)
    return jnp.where(lane < head_dim, values[:, first : first + 1], values[:, first + 1 : first + 2])


def local_kernel(
    x_ref, b_ref, c_ref, step_ref, step_row_ref, log_ref, log_row_ref, start_ref,
    skip_ref, out_ref, end_ref,
):
    tok_rows, inner = x_ref.shape
    head_count = step_ref.shape[1]
    head_dim = inner // head_count
    state_dim = b_ref.shape[1]
    row = lax.broadcasted_iota(jnp.int32, (tok_rows, tok_rows), 0)
    col = lax.broadcasted_iota(jnp.int32, (tok_rows, tok_rows), 1)
    causal = (col >= start_ref[...]) & (col <= row)
    gram = jnp.where(causal, dot(c_ref[...], b_ref[...], ((1,), (1,))), 0.0)
    logs = log_ref[...]
    steps = step_ref[...]
    last_log = logs[tok_rows - 1 :, :]
    last_start = start_ref[tok_rows - 1 :, :]
    place = lax.broadcasted_iota(jnp.int32, (tok_rows, 1), 0)
    weight = jnp.where(place >= last_start, jnp.exp(last_log - logs) * steps, 0.0)
    skip = jnp.broadcast_to(skip_ref[...], (8, head_count))
    for first, span in head_pairs(head_count, head_dim):
        x_pair = x_ref[:, span]
        sides = []
        for head in range(first, min(first + 2, head_count)):
            gap = jnp.minimum(logs[:, head : head + 1] - log_row_ref[head : head + 1, :], 0.0)
            mixing = jnp.exp(gap) * gram * step_row_ref[head : head + 1, :]
            sides.append(dot(mixing.astype(jnp.bfloat16), x_pair))
        x_wide = x_pair.astype(jnp.float32)
        lane = lax.broadcasted_iota(jnp.int32, x_pair.shape, 1)
        out_ref[:, span] = (
            jnp.where(lane < head_dim, sides[0], sides[-1])
            + pair_lanes(skip, first, head_dim)[:1] * x_wide
        )
        weighted = (pair_lanes(weight, first, head_dim) * x_wide).astype(jnp.bfloat16)
        end_ref[:, span] = dot(b_ref[...], weighted, ((0,), (0,))).astype(end_ref.dtype)


def project_kernel(slots, order_ref, *refs):
    prompt_refs = refs[:slots]
    (local_ref, c_ref, pick_ref, inherited_ref, decay_ref, arriving_ref, tail_ref, gate_ref,
     weight_ref, down_ref, up_ref, kept_ref, sent_ref, gated, low_rank) = refs[slots:]
    models, tok_rows, inner = local_ref.shape
    head_count = decay_ref.shape[2]
    head_dim = inner // head_count
    state_dim = c_ref.shape[2]
    share = tok_rows // order_ref.shape[0]
    half = models * tok_rows // 2

    @pl.when(pl.program_id(0) == 0)
    def _():
        for model in range(models):
            c_values = c_ref[model].astype(jnp.float32)
            inherited = inherited_ref[...]
            tail = jnp.broadcast_to(tail_ref[model], (8, head_count))
            mine = dot((c_values * inherited).astype(jnp.bfloat16), arriving_ref[model])
            borrowed = jnp.zeros((tok_rows, inner), jnp.float32)
            for slot in range(0, slots, 4):
                chosen = [c_values * pick_ref[:, i : i + 1] for i in range(slot, slot + 4)]
                states = [prompt_refs[i][model] for i in range(slot, slot + 4)]
                borrowed = borrowed + dot(
                    jnp.concatenate(chosen, axis=1).astype(jnp.bfloat16),
                    jnp.concatenate(states, axis=0),
                )
            decay = decay_ref[model]
            for first, span in head_pairs(head_count, head_dim):
                log_wide = pair_lanes(decay, first, head_dim)
                log_prompt = log_wide + inherited * pair_lanes(tail, first, head_dim)[:1]
                output = (
                    local_ref[model, :, span]
                    + jnp.exp(log_wide) * mine[:, span]
                    + jnp.exp(log_prompt) * borrowed[:, span]
                )
                gate = gate_ref[model, :, span].astype(jnp.float32)
                output = (output * gate / (1.0 + jnp.exp(-gate))).astype(jnp.bfloat16)
                for quarter in range(tok_rows // share):
                    rows = pl.ds(pl.multiple_of(order_ref[quarter] + model * share, share), share)
                    gated[rows, span] = output[quarter * share : (quarter + 1) * share]
        low_rank[...] = dot(gated[...], down_ref[...]).astype(jnp.bfloat16)

    policy = lax.broadcasted_iota(jnp.int32, (models * tok_rows, 1), 0) % (models * share) < share
    adapter = jnp.where(policy, dot(low_rank[...], up_ref[...]), 0.0)
    terms = (dot(gated[...], weight_ref[...]) + adapter).astype(jnp.bfloat16)
    kept_ref[...] = terms[:half]
    sent_ref[...] = terms[half:]


def head_kernel(parts, limit_ref, *refs):
    row_refs = refs[:parts]
    weight_ref, target_ref, out_ref, total = refs[parts:]
    step = pl.program_id(0)
    each = row_refs[0].shape[0]

    @pl.when(step == 0)
    def _():
        total[...] = jnp.zeros_like(total)

    total[...] += dot(jnp.concatenate([rows[...] for rows in row_refs], axis=0), weight_ref[...])

    @pl.when(step == pl.num_programs(0) - 1)
    def _():
        count = total.shape[1]
        for part in range(parts):
            rows = slice(part * each, (part + 1) * each)
            column = lax.broadcasted_iota(jnp.int32, (each, count), 1)
            in_range = column < limit_ref[0]
            logits = jnp.where(in_range, total[rows, :], -jnp.inf)
            top = jnp.max(logits, axis=1, keepdims=True)
            sums = jnp.sum(jnp.exp(logits - top), axis=1, keepdims=True)
            hit = (target_ref[rows, :] - limit_ref[1] == column) & in_range
            target = jnp.sum(jnp.where(hit, logits, 0.0), axis=1, keepdims=True)
            lane = lax.broadcasted_iota(jnp.int32, (each, 128), 1)
            stats = jnp.where(lane == 0, top, jnp.where(lane == 1, sums, target))
            out_ref[:, rows] = jnp.transpose(stats)[:8]


def place_kernel(count, first_ref, *refs):
    whole, held, arrived, left = refs[count:]
    into, out = [], []
    for i in range(count):
        blocks, size = refs[i].shape[:2]
        into.append(pltpu.make_async_copy(refs[i], held.at[i], arrived.at[i]))
        for j in range(blocks):
            rows = pl.ds(pl.multiple_of(first_ref[i * blocks + j], 16), size)
            out.append(
                pltpu.make_async_copy(held.at[i, j], whole.at[rows, :], left.at[i * blocks + j])
            )
    for copy in into:
        copy.start()
    for i in range(count):
        into[i].wait()
        for copy in out[i * blocks : (i + 1) * blocks]:
            copy.start()
    for copy in out:
        copy.wait()


def split_kernel(head_ref, *out_refs):
    size = out_refs[0].shape[0]
    for cut, out_ref in enumerate(out_refs):
        out_ref[...] = head_ref[cut * size : (cut + 1) * size, :]


def cost(flops, moved, exps=0):
    return pl.CostEstimate(flops=flops, bytes_accessed=moved, transcendentals=exps)


def whole_spec():
    return pl.BlockSpec(memory_space=pltpu.VMEM)


def shards(
    scored_token_targets,
    valid,
    lengths,
    owners,
    holders,
    mixer_input_x,
    mixer_gate_input,
    input_projection_b,
    output_projection_c,
    token_step_sizes,
    head_decay_rate,
    head_skip_scale,
    prompt_held_states,
    shared_output_weight,
    adapter_down_weight,
    adapter_up_weight,
    residual,
    final_norm_scale,
    vocab_head_weight,
):
    seq_count = lax.axis_size("seq")
    mp_count = lax.axis_size("mp")
    seq_index = lax.axis_index("seq")
    mp_index = lax.axis_index("mp")
    place = place_of(seq_index)
    core = mp_index % 2
    x_count = mp_count // 2
    x_index = mp_index // 2
    tok_rows = scored_token_targets.shape[0]
    models = mixer_input_x.shape[0]
    inner_local = mixer_input_x.shape[2]
    head_count = token_step_sizes.shape[2]
    state_dim = input_projection_b.shape[2]
    roll_count = lengths.shape[0]
    width = residual.shape[2]
    blocks = seq_count // (CHAIN * SIDE)
    partners = list(itertools.product(range(SIDE), range(blocks)))[1:]
    share_rows = tok_rows // mp_count

    def from_partner(side, block):
        return partner(seq_index, side, blocks - block, seq_count)

    def beside(value):
        return [to_partner(value, side, block) for side, block in partners]

    held = jnp.transpose(prompt_held_states[:, 0], (0, 3, 1, 2)).reshape(
        models, state_dim, inner_local
    )
    states = [held, turn(held, 1), turn(held, 2)]
    states.append(turn(states[2], 1))
    beside_held = beside(held)
    targets = lax.all_gather(
        scored_token_targets, "seq", axis_index_groups=chain_groups(), tiled=False
    )

    first_row = seq_index * tok_rows
    offsets = jnp.arange(tok_rows, dtype=jnp.int32)
    position = first_row + offsets
    starts = jnp.cumsum(lengths) - lengths
    rollout = jnp.sum((starts[None, :] <= position[:, None]).astype(jnp.int32), axis=1) - 1
    member_table = rollout[:, None] == jnp.arange(roll_count, dtype=jnp.int32)[None, :]
    start_local = jnp.sum(jnp.where(member_table, starts[None, :], 0), axis=1) - first_row
    holder_tok = jnp.sum(jnp.where(member_table, holders[None, :], 0), axis=1)
    prompt_holder = jnp.stack(
        [
            turned(source, k)
            for k in range(CHAIN)
            for source in [seq_index] + [from_partner(side, block) for side, block in partners]
        ]
    )
    pick = (holder_tok[:, None] == prompt_holder[None, :]).astype(jnp.float32)
    inherited = (start_local < 0).astype(jnp.float32)
    neg_rates = -head_decay_rate
    log_decay = jnp.cumsum(token_step_sizes * neg_rates[:, None, :], axis=1)
    before = jnp.take(log_decay, jnp.maximum(start_local - 1, 0), axis=1)
    before = jnp.where((start_local >= 1)[None, :, None], before, 0.0)

    mixer_x, states[1], *beside_held = tied(mixer_input_x, states[1], *beside_held)
    per_model = lambda *shape: pl.BlockSpec((None,) + shape, lambda m: (m,) + (0,) * len(shape))
    local_out, local_end = pl.pallas_call(
        local_kernel,
        grid=(models,),
        in_specs=[
            per_model(tok_rows, inner_local),
            per_model(tok_rows, state_dim),
            per_model(tok_rows, state_dim),
            per_model(tok_rows, head_count),
            per_model(head_count, tok_rows),
            per_model(tok_rows, head_count),
            per_model(head_count, tok_rows),
            pl.BlockSpec((tok_rows, 1), lambda m: (0, 0)),
            per_model(1, head_count),
        ],
        out_specs=[per_model(tok_rows, inner_local), per_model(state_dim, inner_local)],
        out_shape=[
            jax.ShapeDtypeStruct((models, tok_rows, inner_local), jnp.float32),
            jax.ShapeDtypeStruct((models, state_dim, inner_local), jnp.bfloat16),
        ],
        compiler_params=pltpu.CompilerParams(vmem_limit_bytes=32 * 2**20),
        cost_estimate=cost(10**9, 8 * 2**20, 2 * 10**6),
        name="local_tokens",
    )(
        mixer_x,
        input_projection_b,
        output_projection_c,
        token_step_sizes,
        jnp.swapaxes(token_step_sizes, 1, 2),
        log_decay,
        jnp.swapaxes(log_decay, 1, 2),
        start_local[:, None],
        head_skip_scale[:, None, :],
    )

    hops = max(1, -(-(seq_count * tok_rows // 8) // tok_rows))
    next_one = [(i, i + 1) for i in range(seq_count - 1)]
    local_tail = log_decay[:, -1] - before[:, -1]
    arriving = lax.ppermute(local_end, "seq", next_one)
    tail = lax.ppermute(local_tail, "seq", next_one)
    if hops > 1:
        through = jnp.repeat(jnp.exp(log_decay[:, -1]), inner_local // head_count, axis=1)
        through = through[:, None, :] * inherited[-1]
        for _ in range(hops - 1):
            moved = through * arriving.astype(jnp.float32) + local_end.astype(jnp.float32)
            arriving = lax.ppermute(moved.astype(jnp.bfloat16), "seq", next_one)
            tail = lax.ppermute(inherited[-1] * tail + local_tail, "seq", next_one)

    head_rows, vocab_local = vocab_head_weight.shape
    part = -(-vocab_local // (CHAIN * 128)) * 128
    cuts = 2 if head_rows % 32 == 0 else 1
    cut_rows = head_rows // cuts
    head = pl.pallas_call(
        split_kernel,
        grid=(CHAIN,),
        in_specs=[pl.BlockSpec((head_rows, part), lambda j: (0, j))],
        out_specs=[pl.BlockSpec((None, cut_rows, part), lambda j: (j, 0, 0))] * cuts,
        out_shape=[jax.ShapeDtypeStruct((CHAIN, cut_rows, part), vocab_head_weight.dtype)] * cuts,
        cost_estimate=cost(0, 2 * vocab_head_weight.size * 2),
        name="split_head_columns",
    )(vocab_head_weight)
    arriving, tail, states[2], states[3], *head = tied(arriving, tail, states[2], states[3], *head)
    came_head = [
        lax.all_to_all(head[cut], "seq", 0, 0, axis_index_groups=chain_groups())
        for cut in range(cuts)
    ]

    prompts = [held] + beside_held
    for state in states[1:]:
        prompts += [state] + beside(state)

    quarter = jnp.arange(mp_count, dtype=jnp.int32)
    order = (quarter % 2 != core) * x_count + (quarter // 2 - x_index) % x_count
    order = order.astype(jnp.int32) * (models * share_rows)
    half = models * tok_rows // 2
    tile = 512 if width % 512 == 0 else width
    kept, sent = pl.pallas_call(
        functools.partial(project_kernel, len(prompts)),
        grid=(width // tile,),
        in_specs=[pl.BlockSpec(memory_space=pltpu.SMEM)]
        + [whole_spec()] * (len(prompts) + 8)
        + [
            pl.BlockSpec((inner_local, tile), lambda j: (0, j)),
            whole_spec(),
            pl.BlockSpec((adapter_up_weight.shape[0], tile), lambda j: (0, j)),
        ],
        out_specs=[pl.BlockSpec((half, tile), lambda j: (0, j))] * 2,
        out_shape=[jax.ShapeDtypeStruct((half, width), jnp.bfloat16)] * 2,
        scratch_shapes=[
            pltpu.VMEM((models * tok_rows, inner_local), jnp.bfloat16),
            pltpu.VMEM((models * tok_rows, adapter_up_weight.shape[0]), jnp.bfloat16),
        ],
        compiler_params=pltpu.CompilerParams(vmem_limit_bytes=48 * 2**20),
        cost_estimate=cost(
            2 * models * tok_rows * inner_local * width, 4 * inner_local * width, 2 * 10**6
        ),
        name="gate_and_project",
    )(
        order,
        *prompts,
        local_out,
        output_projection_c,
        pick,
        inherited[:, None],
        log_decay - before,
        arriving,
        tail[:, None, :],
        mixer_gate_input,
        shared_output_weight,
        adapter_down_weight,
        adapter_up_weight,
    )

    came, targets = tied(other_core(sent), targets)
    each = models * share_rows
    chip_sum = kept.astype(jnp.float32) + came.astype(jnp.float32)
    mixed = chip_sum[:each]
    for by in range(1, x_count):
        away = chip_sum[by * each : (by + 1) * each].astype(jnp.bfloat16)
        mixed = mixed + along_x(away, by).astype(jnp.float32)
    own_rows = lax.dynamic_slice_in_dim(residual, mp_index * share_rows, share_rows, 0)
    hidden = jnp.transpose(own_rows, (1, 0, 2)).reshape(each, width).astype(jnp.float32) + mixed
    mean_sq = jnp.mean(hidden * hidden, axis=-1, keepdims=True)
    normed_own = (hidden * lax.rsqrt(mean_sq + 1e-05) * final_norm_scale).astype(jnp.bfloat16)

    came_head[-1], _ = tied(came_head[-1], normed_own)
    rows_of = [normed_own, turn(normed_own, 1), turn(normed_own, 2)]
    pieces, firsts = [], []
    for cut in range(cuts):
        sources = [seq_index] + [from_partner(side, block) for side, block in partners]
        pieces += [came_head[cut]] + beside(came_head[cut])
        for source in sources:
            first_of_chain = source - place_of(source) * SIDE
            firsts += [
                (first_of_chain + k * SIDE) * head_rows + cut * cut_rows for k in range(CHAIN)
            ]
    head_part = pl.pallas_call(
        functools.partial(place_kernel, len(pieces)),
        in_specs=[pl.BlockSpec(memory_space=pltpu.SMEM)]
        + [pl.BlockSpec(memory_space=pl.ANY)] * len(pieces),
        out_specs=pl.BlockSpec(memory_space=pl.ANY),
        out_shape=jax.ShapeDtypeStruct((seq_count * head_rows, part), vocab_head_weight.dtype),
        scratch_shapes=[
            pltpu.VMEM((len(pieces), CHAIN, cut_rows, part), vocab_head_weight.dtype),
            pltpu.SemaphoreType.DMA((len(pieces),)),
            pltpu.SemaphoreType.DMA((len(pieces) * CHAIN,)),
        ],
        compiler_params=pltpu.CompilerParams(vmem_limit_bytes=16 * 2**20),
        cost_estimate=cost(0, 4 * seq_count * head_rows * part),
        name="place_head_rows",
    )(jnp.stack(firsts).astype(jnp.int32), *pieces)
    last_rows, head_part = tied(turn(rows_of[2], 1), head_part)
    rows_of.append(last_rows)

    limit = jnp.stack(
        [
            jnp.minimum(vocab_local - place * part, part),
            mp_index * vocab_local + place * part,
        ]
    ).astype(jnp.int32)
    depth = 512 if width % 512 == 0 else width
    parts = mp_count
    chain_stats = []
    mp_order = jnp.stack(
        [(x_index - k) % x_count * 2 + (core + other) % 2 for other in (0, 1) for k in range(x_count)]
    )
    def head_stats(rows, targets):
        near = [rows] + [along_x(rows, by) for by in range(1, x_count)]
        all_rows = near + [other_core(value) for value in near]
        targets = jnp.repeat(targets.reshape(mp_count, 1, share_rows)[mp_order], models, axis=1)
        stats = pl.pallas_call(
            functools.partial(head_kernel, parts),
            grid=(width // depth,),
            in_specs=[pl.BlockSpec(memory_space=pltpu.SMEM)]
            + [pl.BlockSpec((each, depth), lambda j: (0, j))] * parts
            + [pl.BlockSpec((depth, part), lambda j: (j, 0)), whole_spec()],
            out_specs=whole_spec(),
            out_shape=jax.ShapeDtypeStruct((8, parts * each), jnp.float32),
            scratch_shapes=[pltpu.VMEM((parts * each, part), jnp.float32)],
            compiler_params=pltpu.CompilerParams(vmem_limit_bytes=48 * 2**20),
            cost_estimate=cost(
                2 * parts * each * width * part, 2 * (parts * each + part) * width, parts * each * part
            ),
            name="head_stats",
        )(limit, *all_rows, head_part, targets.reshape(parts * each, 1))
        return stats.reshape(8, 2, x_count, models, share_rows)

    for k in range(CHAIN):
        stats = head_stats(rows_of[k], targets[place ^ k])
        chain_stats.append(stats if k == 0 else turn(stats, k))

    def merged(several):
        top = functools.reduce(jnp.maximum, [stats[0] for stats in several])
        total = sum(stats[1] * jnp.exp(stats[0] - top) for stats in several)
        return jnp.stack([top, total, sum(stats[2] for stats in several)])

    stats = merged(chain_stats)
    stats = merged([stats, other_core(stats)[:, ::-1]])
    stats = merged(
        [stats] + [jnp.roll(along_x(stats, by), by, axis=2) for by in range(1, x_count)]
    )
    logprob = stats[2] - stats[0] - jnp.log(stats[1])
    delta = (logprob[:, :, 0] - logprob[:, :, 1]).reshape(mp_count, share_rows)
    token_delta = jnp.sum(
        jnp.where(mp_order[None, :, None] == quarter[:, None, None], delta[None], 0.0), axis=1
    ).reshape(tok_rows)
    token_delta = token_delta * valid.astype(jnp.float32)
    roll_sums = jnp.dot(token_delta, member_table.astype(jnp.float32), precision=highest)
    distance = 1
    while distance < seq_count:
        pairs = [(i, i ^ distance) for i in range(seq_count)]
        roll_sums = roll_sums + lax.ppermute(roll_sums, "seq", pairs)
        distance *= 2
    owner_sums = jnp.where(owners == seq_index, roll_sums / lengths.astype(jnp.float32), 0.0)
    return (owner_sums[None, :], token_delta)


def solution(mesh):
    placed = (
        P("seq"),
        P("seq"),
        P(),
        P(),
        P(),
        P(None, "seq", "mp"),
        P(None, "seq", "mp"),
        P(None, "seq", None),
        P(None, "seq", None),
        P(None, "seq", "mp"),
        P(None, "mp"),
        P(None, "mp"),
        P(None, "seq", "mp", None, None),
        P("mp", None),
        P("mp", None),
        P(),
        P("seq", None, None),
        P(),
        P("seq", "mp"),
    )
    return jax.shard_map(
        shards, mesh=mesh, in_specs=placed, out_specs=(P("seq", None), P("seq")), check_vma=False
    )
```

```python
import functools
import itertools

import jax
import jax.numpy as jnp
from jax import lax
from jax.experimental import pallas as pl
from jax.experimental.pallas import tpu as pltpu
from jax.sharding import PartitionSpec as P

highest = lax.Precision.HIGHEST
CHAIN = 4
SIDE = 2


def place_of(i):
    return (i // SIDE) % CHAIN


def turned(i, by):
    return i ^ (by * SIDE)


def partner(i, side, block, count):
    return ((i ^ side) + block * CHAIN * SIDE) % count


def turn(x, by):
    count = lax.axis_size("seq")
    return lax.ppermute(x, "seq", [(i, turned(i, by)) for i in range(count)])


def to_partner(x, side, block):
    count = lax.axis_size("seq")
    return lax.ppermute(x, "seq", [(i, partner(i, side, block, count)) for i in range(count)])


def passed_on(up, down, step):
    count = lax.axis_size("seq")
    ups = [(i, i + SIDE) for i in range(count) if step - 1 <= place_of(i) < CHAIN - 1]
    downs = [(i, i - SIDE) for i in range(count) if 0 < place_of(i) <= CHAIN - step]
    return lax.ppermute(up, "seq", ups), lax.ppermute(down, "seq", downs)


def chain_groups():
    count = lax.axis_size("seq")
    return [
        [first + k * SIDE for k in range(CHAIN)] for first in range(count) if place_of(first) == 0
    ]


def other_core(x):
    count = lax.axis_size("mp")
    return lax.ppermute(x, "mp", [(i, i ^ 1) for i in range(count)])


def along_x(x, by):
    count = lax.axis_size("mp")
    return lax.ppermute(x, "mp", [(i, (i + 2 * by) % count) for i in range(count)])


def tied(*values):
    return lax.optimization_barrier(values)


def dot(a, b, over=((1,), (0,))):
    return lax.dot_general(a, b, (over, ((), ())), preferred_element_type=jnp.float32)


def exact(a, b):
    return lax.dot_general(
        a, b, (((1,), (0,)), ((), ())), precision=highest, preferred_element_type=jnp.float32
    )


def head_pairs(head_count, head_dim):
    return [
        (first, slice(first * head_dim, min(first + 2, head_count) * head_dim))
        for first in range(0, head_count, 2)
    ]


def pair_lanes(values, first, head_dim):
    if first + 1 == values.shape[1]:
        return jnp.broadcast_to(values[:, first : first + 1], (values.shape[0], head_dim))
    lane = lax.broadcasted_iota(jnp.int32, (values.shape[0], 2 * head_dim), 1)
    return jnp.where(lane < head_dim, values[:, first : first + 1], values[:, first + 1 : first + 2])


def local_kernel(
    x_ref, b_ref, c_ref, step_ref, rate_ref, start_ref, skip_ref, out_ref, end_ref, decay_ref,
):
    tok_rows, inner = x_ref.shape
    head_count = step_ref.shape[1]
    head_dim = inner // head_count
    state_dim = b_ref.shape[1]
    row = lax.broadcasted_iota(jnp.int32, (tok_rows, tok_rows), 0)
    col = lax.broadcasted_iota(jnp.int32, (tok_rows, tok_rows), 1)
    causal = (col >= start_ref[...]) & (col <= row)
    gram = jnp.where(causal, dot(c_ref[...], b_ref[...], ((1,), (1,))), 0.0)
    steps = step_ref[...]
    logs = exact(jnp.where(col <= row, 1.0, 0.0), -steps * rate_ref[...])
    decay_ref[...] = logs - exact(jnp.where(col == start_ref[...] - 1, 1.0, 0.0), logs)
    fill = jnp.zeros((tok_rows, 128 - 2 * head_count), jnp.float32)
    as_rows = jnp.transpose(jnp.concatenate([logs, steps, fill], axis=1))
    last_log = logs[tok_rows - 1 :, :]
    last_start = start_ref[tok_rows - 1 :, :]
    place = lax.broadcasted_iota(jnp.int32, (tok_rows, 1), 0)
    weight = jnp.where(place >= last_start, jnp.exp(last_log - logs) * steps, 0.0)
    skip = jnp.broadcast_to(skip_ref[...], (8, head_count))
    for first, span in head_pairs(head_count, head_dim):
        x_pair = x_ref[:, span]
        sides = []
        for head in range(first, min(first + 2, head_count)):
            gap = jnp.minimum(logs[:, head : head + 1] - as_rows[head : head + 1, :], 0.0)
            mixing = jnp.exp(gap) * gram * as_rows[head_count + head : head_count + head + 1, :]
            sides.append(dot(mixing.astype(jnp.bfloat16), x_pair))
        x_wide = x_pair.astype(jnp.float32)
        lane = lax.broadcasted_iota(jnp.int32, x_pair.shape, 1)
        out_ref[:, span] = (
            jnp.where(lane < head_dim, sides[0], sides[-1])
            + pair_lanes(skip, first, head_dim)[:1] * x_wide
        )
        weighted = (pair_lanes(weight, first, head_dim) * x_wide).astype(jnp.bfloat16)
        end_ref[:, span] = dot(b_ref[...], weighted, ((0,), (0,))).astype(end_ref.dtype)


def project_kernel(slots, order_ref, *refs):
    prompt_refs = refs[:slots]
    (local_ref, c_ref, pick_ref, inherited_ref, decay_ref, arriving_ref, tail_ref, gate_ref,
     weight_ref, down_ref, up_ref, kept_ref, sent_ref, gated, low_rank) = refs[slots:]
    models, tok_rows, inner = local_ref.shape
    head_count = decay_ref.shape[2]
    head_dim = inner // head_count
    state_dim = c_ref.shape[2]
    share = tok_rows // order_ref.shape[0]
    half = models * tok_rows // 2

    @pl.when(pl.program_id(0) == 0)
    def _():
        for model in range(models):
            c_values = c_ref[model].astype(jnp.float32)
            inherited = inherited_ref[...]
            tail = jnp.broadcast_to(tail_ref[model], (8, head_count))
            mine = dot((c_values * inherited).astype(jnp.bfloat16), arriving_ref[model])
            borrowed = jnp.zeros((tok_rows, inner), jnp.float32)
            for slot in range(0, slots, 4):
                chosen = [c_values * pick_ref[:, i : i + 1] for i in range(slot, slot + 4)]
                states = [prompt_refs[i][model] for i in range(slot, slot + 4)]
                borrowed = borrowed + dot(
                    jnp.concatenate(chosen, axis=1).astype(jnp.bfloat16),
                    jnp.concatenate(states, axis=0),
                )
            decay = decay_ref[model]
            for first, span in head_pairs(head_count, head_dim):
                log_wide = pair_lanes(decay, first, head_dim)
                log_prompt = log_wide + inherited * pair_lanes(tail, first, head_dim)[:1]
                output = (
                    local_ref[model, :, span]
                    + jnp.exp(log_wide) * mine[:, span]
                    + jnp.exp(log_prompt) * borrowed[:, span]
                )
                gate = gate_ref[model, :, span].astype(jnp.float32)
                output = (output * gate / (1.0 + jnp.exp(-gate))).astype(jnp.bfloat16)
                for quarter in range(tok_rows // share):
                    rows = pl.ds(pl.multiple_of(order_ref[quarter] + model * share, share), share)
                    gated[rows, span] = output[quarter * share : (quarter + 1) * share]
        low_rank[...] = dot(gated[...], down_ref[...]).astype(jnp.bfloat16)

    policy = lax.broadcasted_iota(jnp.int32, (models * tok_rows, 1), 0) % (models * share) < share
    adapter = jnp.where(policy, dot(low_rank[...], up_ref[...]), 0.0)
    terms = (dot(gated[...], weight_ref[...]) + adapter).astype(jnp.bfloat16)
    kept_ref[...] = terms[:half]
    sent_ref[...] = terms[half:]


def head_kernel(parts, limit_ref, *refs):
    row_refs = refs[:parts]
    weight_ref, target_ref, out_ref, held, logits_ref, arrived = refs[parts:]
    each = row_refs[0].shape[0]
    tiles, _, tile = held.shape
    copies = [
        pltpu.make_async_copy(
            weight_ref.at[:, pl.ds(i * tile, tile)], held.at[i], arrived.at[i]
        )
        for i in range(tiles)
    ]
    for copy in copies:
        copy.start()
    spans = [slice(part * each, (part + 1) * each) for part in range(parts)]
    for i in range(tiles):
        copies[i].wait()
        for rows, row_ref in zip(spans, row_refs):
            logits_ref[rows, i * tile : (i + 1) * tile] = dot(row_ref[...], held[i])
    for rows in spans:
        logits = logits_ref[rows, :]
        column = lax.broadcasted_iota(jnp.int32, logits.shape, 1)
        in_range = column < limit_ref[0]
        logits = jnp.where(in_range, logits, -jnp.inf)
        top = jnp.max(logits, axis=1, keepdims=True)
        sums = jnp.sum(jnp.exp(logits - top), axis=1, keepdims=True)
        hit = (target_ref[rows, :] - limit_ref[1] == column) & in_range
        target = jnp.sum(jnp.where(hit, logits, 0.0), axis=1, keepdims=True)
        lane = lax.broadcasted_iota(jnp.int32, (each, 128), 1)
        stats = jnp.where(lane == 0, top, jnp.where(lane == 1, sums, target))
        out_ref[:, rows] = jnp.transpose(stats)[:8]


def place_kernel(count, first_ref, *refs):
    whole, arrived = refs[count:]
    copies = []
    for i in range(count):
        blocks, size = refs[i].shape[:2]
        for j in range(blocks):
            rows = pl.ds(pl.multiple_of(first_ref[i * blocks + j], 16), size)
            copies.append(
                pltpu.make_async_copy(
                    refs[i].at[j], whole.at[rows, :], arrived.at[i * blocks + j]
                )
            )
    for copy in copies:
        copy.start()
    for copy in copies:
        copy.wait()


def split_kernel(head_ref, *out_refs):
    size = out_refs[0].shape[0]
    for cut, out_ref in enumerate(out_refs):
        out_ref[...] = head_ref[cut * size : (cut + 1) * size, :]


def cost(flops, moved, exps=0):
    return pl.CostEstimate(flops=flops, bytes_accessed=moved, transcendentals=exps)


def whole(value):
    return pl.BlockSpec(value.shape, lambda *_: (0,) * value.ndim)


def across(x, by):
    count = lax.axis_size("mp")
    return lax.ppermute(x, "mp", [(i, (i + 2 * by) % count ^ 1) for i in range(count)])


def shards(
    scored_token_targets,
    valid,
    lengths,
    owners,
    holders,
    mixer_input_x,
    mixer_gate_input,
    input_projection_b,
    output_projection_c,
    token_step_sizes,
    head_decay_rate,
    head_skip_scale,
    prompt_held_states,
    shared_output_weight,
    adapter_down_weight,
    adapter_up_weight,
    residual,
    final_norm_scale,
    vocab_head_weight,
):
    seq_count = lax.axis_size("seq")
    mp_count = lax.axis_size("mp")
    seq_index = lax.axis_index("seq")
    mp_index = lax.axis_index("mp")
    place = place_of(seq_index)
    core = mp_index % 2
    x_count = mp_count // 2
    x_index = mp_index // 2
    tok_rows = scored_token_targets.shape[0]
    models = mixer_input_x.shape[0]
    inner_local = mixer_input_x.shape[2]
    head_count = token_step_sizes.shape[2]
    state_dim = input_projection_b.shape[2]
    roll_count = lengths.shape[0]
    width = residual.shape[2]
    blocks = seq_count // (CHAIN * SIDE)
    partners = list(itertools.product(range(SIDE), range(blocks)))[1:]
    share_rows = tok_rows // mp_count

    def from_partner(side, block):
        return partner(seq_index, side, blocks - block, seq_count)

    def beside(value):
        return [to_partner(value, side, block) for side, block in partners]

    held = jnp.transpose(prompt_held_states[:, 0], (0, 3, 1, 2)).reshape(
        models, state_dim, inner_local
    )
    states = [held, turn(held, 1), turn(held, 2)]
    states.append(turn(states[2], 1))
    beside_held = beside(held)

    first_row = seq_index * tok_rows
    offsets = jnp.arange(tok_rows, dtype=jnp.int32)
    position = first_row + offsets
    starts = jnp.cumsum(lengths) - lengths
    rollout = jnp.sum((starts[None, :] <= position[:, None]).astype(jnp.int32), axis=1) - 1
    member_table = rollout[:, None] == jnp.arange(roll_count, dtype=jnp.int32)[None, :]
    start_local = jnp.sum(jnp.where(member_table, starts[None, :], 0), axis=1) - first_row
    holder_tok = jnp.sum(jnp.where(member_table, holders[None, :], 0), axis=1)
    prompt_holder = jnp.stack(
        [
            turned(source, k)
            for k in range(CHAIN)
            for source in [seq_index] + [from_partner(side, block) for side, block in partners]
        ]
    )
    last_rollout = (offsets >= start_local[-1]).astype(jnp.float32)
    local_tail = -head_decay_rate * jnp.sum(
        token_step_sizes * last_rollout[None, :, None], axis=1
    )
    next_one = [(i, i + 1) for i in range(seq_count - 1)]
    tail = lax.ppermute(local_tail, "seq", next_one)
    pick = (holder_tok[:, None] == prompt_holder[None, :]).astype(jnp.float32)
    inherited = (start_local < 0).astype(jnp.float32)
    beside_next = beside(states[1])
    mixer_x, states[1], tail, *beside_held = tied(
        mixer_input_x, states[1], tail, *beside_held
    )

    per_model = lambda *shape: pl.BlockSpec((None,) + shape, lambda m: (m,) + (0,) * len(shape))
    local_out, local_end, decay = pl.pallas_call(
        local_kernel,
        grid=(models,),
        in_specs=[
            per_model(tok_rows, inner_local),
            per_model(tok_rows, state_dim),
            per_model(tok_rows, state_dim),
            per_model(tok_rows, head_count),
            per_model(1, head_count),
            pl.BlockSpec((tok_rows, 1), lambda m: (0, 0)),
            per_model(1, head_count),
        ],
        out_specs=[
            per_model(tok_rows, inner_local),
            per_model(state_dim, inner_local),
            per_model(tok_rows, head_count),
        ],
        out_shape=[
            jax.ShapeDtypeStruct((models, tok_rows, inner_local), jnp.float32),
            jax.ShapeDtypeStruct((models, state_dim, inner_local), jnp.bfloat16),
            jax.ShapeDtypeStruct((models, tok_rows, head_count), jnp.float32),
        ],
        compiler_params=pltpu.CompilerParams(vmem_limit_bytes=32 * 2**20),
        cost_estimate=cost(10**9, 8 * 2**20, 2 * 10**6),
        name="local_tokens",
    )(
        mixer_x,
        input_projection_b,
        output_projection_c,
        token_step_sizes,
        head_decay_rate[:, None, :],
        start_local[:, None],
        head_skip_scale[:, None, :],
    )

    hops = max(1, -(-(seq_count * tok_rows // 8) // tok_rows))
    arriving = lax.ppermute(local_end, "seq", next_one)
    if hops > 1:
        through = jnp.repeat(jnp.exp(local_tail), inner_local // head_count, axis=1)
        through = through[:, None, :] * inherited[-1]
        for _ in range(hops - 1):
            moved = through * arriving.astype(jnp.float32) + local_end.astype(jnp.float32)
            arriving = lax.ppermute(moved.astype(jnp.bfloat16), "seq", next_one)
            tail = lax.ppermute(inherited[-1] * tail + local_tail, "seq", next_one)

    head_rows, vocab_local = vocab_head_weight.shape
    part = -(-vocab_local // (CHAIN * 128)) * 128
    cuts = 2 if head_rows % 32 == 0 else 1
    cut_rows = head_rows // cuts
    head = pl.pallas_call(
        split_kernel,
        grid=(CHAIN,),
        in_specs=[pl.BlockSpec((head_rows, part), lambda j: (0, j))],
        out_specs=[pl.BlockSpec((None, cut_rows, part), lambda j: (j, 0, 0))] * cuts,
        out_shape=[jax.ShapeDtypeStruct((CHAIN, cut_rows, part), vocab_head_weight.dtype)] * cuts,
        cost_estimate=cost(0, 2 * vocab_head_weight.size * 2),
        name="split_head_columns",
    )(vocab_head_weight)
    targets = jnp.stack([scored_token_targets, turn(scored_token_targets, 1)])
    targets = jnp.concatenate([targets, turn(targets, 2)])
    arriving, states[3], targets, *head = tied(arriving, states[3], targets, *head)
    came_head = [
        lax.all_to_all(head[cut], "seq", 0, 0, axis_index_groups=chain_groups())
        for cut in range(cuts)
    ]

    besides = [beside_held, beside_next, beside(states[2]), beside(states[3])]
    prompts = []
    for state, others in zip(states, besides):
        prompts += [state] + list(others)

    quarter = jnp.arange(mp_count, dtype=jnp.int32)
    order = (quarter % 2 != core) * x_count + (quarter // 2 - x_index) % x_count
    order = order.astype(jnp.int32) * (models * share_rows)
    half = models * tok_rows // 2
    tile = 512 if width % 512 == 0 else width
    resident = [
        *prompts,
        local_out,
        output_projection_c,
        pick,
        inherited[:, None],
        decay,
        arriving,
        tail[:, None, :],
        mixer_gate_input,
    ]
    kept, sent = pl.pallas_call(
        functools.partial(project_kernel, len(prompts)),
        grid=(width // tile,),
        in_specs=[pl.BlockSpec(memory_space=pltpu.SMEM)]
        + [whole(value) for value in resident]
        + [
            pl.BlockSpec((inner_local, tile), lambda j: (0, j)),
            whole(adapter_down_weight),
            pl.BlockSpec((adapter_up_weight.shape[0], tile), lambda j: (0, j)),
        ],
        out_specs=[pl.BlockSpec((half, tile), lambda j: (0, j))] * 2,
        out_shape=[jax.ShapeDtypeStruct((half, width), jnp.bfloat16)] * 2,
        scratch_shapes=[
            pltpu.VMEM((models * tok_rows, inner_local), jnp.bfloat16),
            pltpu.VMEM((models * tok_rows, adapter_up_weight.shape[0]), jnp.bfloat16),
        ],
        compiler_params=pltpu.CompilerParams(vmem_limit_bytes=56 * 2**20),
        cost_estimate=cost(
            2 * models * tok_rows * inner_local * width, 4 * inner_local * width, 2 * 10**6
        ),
        name="gate_and_project",
    )(order, *resident, shared_output_weight, adapter_down_weight, adapter_up_weight)

    sent, came_head[0] = tied(sent, came_head[0])
    came = other_core(sent)
    each = models * share_rows

    def chip_sum(by):
        rows = slice(by * each, (by + 1) * each)
        return kept[rows].astype(jnp.float32) + came[rows].astype(jnp.float32)

    mixed = chip_sum(0)
    for by in range(1, x_count):
        mixed = mixed + along_x(chip_sum(by).astype(jnp.bfloat16), by).astype(jnp.float32)
    besides_head = [beside(came_head[0])]
    mixed, came_head[-1], *besides_head[0] = tied(mixed, came_head[-1], *besides_head[0])
    own_rows = lax.dynamic_slice_in_dim(residual, mp_index * share_rows, share_rows, 0)
    hidden = jnp.transpose(own_rows, (1, 0, 2)).reshape(each, width).astype(jnp.float32) + mixed
    mean_sq = jnp.mean(hidden * hidden, axis=-1, keepdims=True)
    normed_own = (hidden * lax.rsqrt(mean_sq + 1e-05) * final_norm_scale).astype(jnp.bfloat16)

    limit = jnp.stack(
        [
            jnp.minimum(vocab_local - place * part, part),
            mp_index * vocab_local + place * part,
        ]
    ).astype(jnp.int32)
    mp_order = jnp.stack(
        [(x_index - k) % x_count * 2 + (core + other) % 2 for other in (0, 1) for k in range(x_count)]
    )

    def words_of(targets):
        targets = targets.reshape(CHAIN, mp_count, 1, share_rows)[:, mp_order]
        targets = jnp.broadcast_to(targets, (CHAIN, mp_count, models, share_rows))
        return targets.reshape(CHAIN, 2, x_count, each)

    tiles = 2 if part % 256 == 0 else 1

    def place_head():
        pieces, firsts = [], []
        for cut, others in enumerate(besides_head):
            pieces += [came_head[cut]] + others
            for source in [seq_index] + [from_partner(side, block) for side, block in partners]:
                first_of_chain = source - place_of(source) * SIDE
                firsts += [
                    (first_of_chain + k * SIDE) * head_rows + cut * cut_rows for k in range(CHAIN)
                ]
        return pl.pallas_call(
            functools.partial(place_kernel, len(pieces)),
            in_specs=[pl.BlockSpec(memory_space=pltpu.SMEM)]
            + [pl.BlockSpec(memory_space=pl.ANY)] * len(pieces),
            out_specs=pl.BlockSpec(memory_space=pltpu.VMEM),
            out_shape=jax.ShapeDtypeStruct((seq_count * head_rows, part), vocab_head_weight.dtype),
            scratch_shapes=[pltpu.SemaphoreType.DMA((len(pieces) * CHAIN,))],
            compiler_params=pltpu.CompilerParams(vmem_limit_bytes=16 * 2**20),
            cost_estimate=cost(0, 4 * seq_count * head_rows * part),
            name="place_head_rows",
        )(jnp.stack(firsts).astype(jnp.int32), *pieces)

    def head_stats(head_part, rows, words):
        count = len(rows)
        words = words.reshape(count * each, 1)
        stats_shape = jax.ShapeDtypeStruct((8, count * each), jnp.float32)
        return pl.pallas_call(
            functools.partial(head_kernel, count),
            in_specs=[pl.BlockSpec(memory_space=pltpu.SMEM)]
            + [pl.BlockSpec(memory_space=pltpu.VMEM)] * count
            + [pl.BlockSpec(memory_space=pl.ANY), pl.BlockSpec(memory_space=pltpu.VMEM)],
            out_specs=pl.BlockSpec(memory_space=pltpu.VMEM),
            out_shape=stats_shape,
            scratch_shapes=[
                pltpu.VMEM((tiles, width, part // tiles), jnp.bfloat16),
                pltpu.VMEM((count * each, part), jnp.float32),
                pltpu.SemaphoreType.DMA((tiles,)),
            ],
            compiler_params=pltpu.CompilerParams(vmem_limit_bytes=56 * 2**20),
            cost_estimate=cost(
                2 * count * each * width * part,
                2 * (count * each + part) * width,
                count * each * part,
            ),
            name="head_stats",
        )(limit, *rows, head_part, words).reshape(8, count, models, share_rows)

    def both_cores(values):
        return values + [other_core(value) for value in values]

    def crossed(rows):
        return [along_x(rows, by) for by in range(1, x_count)]

    halves = [came_head[-1][: CHAIN // 2], came_head[-1][CHAIN // 2 :]] if cuts == 2 else []
    blocks_of = [normed_own]
    nears = [crossed(normed_own)]
    up, down = normed_own, normed_own
    ups, downs, late = [], [], []
    words = words_of(targets)
    for step in range(1, CHAIN):
        up, down = passed_on(up, down, step)
        count = len(nears[-1])
        extra = []
        if step <= len(halves):
            late.append(beside(halves[step - 1]))
            extra = late[-1]
        if step == CHAIN - 2:
            if cuts == 2:
                besides_head.append([jnp.concatenate(both) for both in zip(late[0], late[1])])
            extra = [place_head()]
        elif step == CHAIN - 1:
            rows = [both_cores([blocks_of[k]] + nears[k]) for k in (0, 1)]
            extra = [head_stats(head_part, rows[0] + rows[1], words[:2])]
        up, down, *came = tied(up, down, *nears[-1], *extra)
        nears[-1], extra = came[:count], came[count:]
        if step <= len(halves) and step < CHAIN - 2:
            late[-1] = extra
        elif step == CHAIN - 2:
            head_part = extra[0]
        elif step == CHAIN - 1:
            early = extra[0]
        ups.append(up)
        downs.append(down)
        if step == 1:
            block = jnp.where(place % 2 == 1, up, down)
        elif step == 2:
            block = jnp.where(place >= 2, up, down)
        else:
            near = jnp.where(place == 1, downs[0], ups[0])
            block = jnp.where(place == 0, down, jnp.where(place == 3, up, near))
        blocks_of.append(block)
        nears.append(crossed(block))

    last = CHAIN - 1
    middle = head_stats(
        head_part,
        both_cores([blocks_of[last - 1]] + nears[last - 1]) + both_cores([blocks_of[last]]),
        jnp.concatenate([words[last - 1].reshape(-1, each), words[last, :, 0]]),
    )
    *nears[last], early, middle = tied(*nears[last], early, middle)
    rest = head_stats(head_part, both_cores(nears[last]), words[last, :, 1:])
    grid_shape = (8, 2, x_count, models, share_rows)
    stats_of = [
        early[:, :mp_count].reshape(grid_shape),
        early[:, mp_count:].reshape(grid_shape),
        middle[:, :mp_count].reshape(grid_shape),
        jnp.concatenate(
            [
                middle[:, mp_count:].reshape(8, 2, 1, models, share_rows),
                rest.reshape(8, 2, x_count - 1, models, share_rows),
            ],
            axis=2,
        ),
    ]
    chain_stats = [stats_of[0]] + [turn(stats_of[k], k) for k in range(1, CHAIN)]

    def merged(several):
        top = functools.reduce(jnp.maximum, [stats[0] for stats in several])
        total = sum(stats[1] * jnp.exp(stats[0] - top) for stats in several)
        return jnp.stack([top, total, sum(stats[2] for stats in several)])

    stats = merged(chain_stats)
    several = [stats, other_core(stats)[:, ::-1]]
    for by in range(1, x_count):
        several.append(jnp.roll(along_x(stats, by), by, axis=2))
        several.append(jnp.roll(across(stats, by)[:, ::-1], by, axis=2))
    stats = merged(several)
    logprob = stats[2] - stats[0] - jnp.log(stats[1])
    delta = (logprob[:, :, 0] - logprob[:, :, 1]).reshape(mp_count, share_rows)
    token_delta = jnp.sum(
        jnp.where(mp_order[None, :, None] == quarter[:, None, None], delta[None], 0.0), axis=1
    ).reshape(tok_rows)
    token_delta = token_delta * valid.astype(jnp.float32)
    roll_sums = jnp.dot(token_delta, member_table.astype(jnp.float32), precision=highest)
    roll_sums = roll_sums + sum(turn(roll_sums, k) for k in range(1, CHAIN))
    roll_sums = roll_sums + sum(beside(roll_sums))
    owner_sums = jnp.where(owners == seq_index, roll_sums / lengths.astype(jnp.float32), 0.0)
    return (owner_sums[None, :], token_delta)


def solution(mesh):
    placed = (
        P("seq"),
        P("seq"),
        P(),
        P(),
        P(),
        P(None, "seq", "mp"),
        P(None, "seq", "mp"),
        P(None, "seq", None),
        P(None, "seq", None),
        P(None, "seq", "mp"),
        P(None, "mp"),
        P(None, "mp"),
        P(None, "seq", "mp", None, None),
        P("mp", None),
        P("mp", None),
        P(),
        P("seq", None, None),
        P(),
        P("seq", "mp"),
    )
    return jax.shard_map(
        shards, mesh=mesh, in_specs=placed, out_specs=(P("seq", None), P("seq")), check_vma=False
    )
```

```python
import functools
import itertools

import jax
import jax.numpy as jnp
from jax import lax
from jax.experimental import pallas as pl
from jax.experimental.pallas import tpu as pltpu
from jax.sharding import PartitionSpec as P

highest = lax.Precision.HIGHEST
CHAIN = 4
SIDE = 2


def place_of(i):
    return (i // SIDE) % CHAIN


def turned(i, by):
    return i ^ (by * SIDE)


def partner(i, side, block, count):
    return ((i ^ side) + block * CHAIN * SIDE) % count


def turn(x, by):
    count = lax.axis_size("seq")
    return lax.ppermute(x, "seq", [(i, turned(i, by)) for i in range(count)])


def to_partner(x, side, block):
    count = lax.axis_size("seq")
    return lax.ppermute(x, "seq", [(i, partner(i, side, block, count)) for i in range(count)])


def between(x, pairs):
    count = lax.axis_size("seq")
    sends = [
        (i, i + (to - place) * SIDE)
        for i in range(count)
        for place, to in pairs
        if place_of(i) == place
    ]
    return lax.ppermute(x, "seq", sends)


def chain_groups():
    count = lax.axis_size("seq")
    return [
        [first + k * SIDE for k in range(CHAIN)] for first in range(count) if place_of(first) == 0
    ]


def other_core(x):
    count = lax.axis_size("mp")
    return lax.ppermute(x, "mp", [(i, i ^ 1) for i in range(count)])


def along_x(x, by):
    count = lax.axis_size("mp")
    return lax.ppermute(x, "mp", [(i, (i + 2 * by) % count) for i in range(count)])


def tied(*values):
    return list(lax.optimization_barrier(values))


def dot(a, b, over=((1,), (0,))):
    return lax.dot_general(a, b, (over, ((), ())), preferred_element_type=jnp.float32)


def exact(a, b):
    return lax.dot_general(
        a, b, (((1,), (0,)), ((), ())), precision=highest, preferred_element_type=jnp.float32
    )


def head_pairs(head_count, head_dim):
    return [
        (first, slice(first * head_dim, min(first + 2, head_count) * head_dim))
        for first in range(0, head_count, 2)
    ]


def pair_lanes(values, first, head_dim):
    if first + 1 == values.shape[1]:
        return jnp.broadcast_to(values[:, first : first + 1], (values.shape[0], head_dim))
    lane = lax.broadcasted_iota(jnp.int32, (values.shape[0], 2 * head_dim), 1)
    return jnp.where(lane < head_dim, values[:, first : first + 1], values[:, first + 1 : first + 2])


def local_kernel(
    x_ref, b_ref, c_ref, step_ref, rate_ref, start_ref, skip_ref, out_ref, end_ref, decay_ref,
):
    tok_rows, inner = x_ref.shape
    head_count = step_ref.shape[1]
    head_dim = inner // head_count
    state_dim = b_ref.shape[1]
    row = lax.broadcasted_iota(jnp.int32, (tok_rows, tok_rows), 0)
    col = lax.broadcasted_iota(jnp.int32, (tok_rows, tok_rows), 1)
    causal = (col >= start_ref[...]) & (col <= row)
    gram = jnp.where(causal, dot(c_ref[...], b_ref[...], ((1,), (1,))), 0.0)
    steps = step_ref[...]
    logs = exact(jnp.where(col <= row, 1.0, 0.0), -steps * rate_ref[...])
    decay_ref[...] = logs - exact(jnp.where(col == start_ref[...] - 1, 1.0, 0.0), logs)
    fill = jnp.zeros((tok_rows, 128 - 2 * head_count), jnp.float32)
    as_rows = jnp.transpose(jnp.concatenate([logs, steps, fill], axis=1))
    last_log = logs[tok_rows - 1 :, :]
    last_start = start_ref[tok_rows - 1 :, :]
    place = lax.broadcasted_iota(jnp.int32, (tok_rows, 1), 0)
    weight = jnp.where(place >= last_start, jnp.exp(last_log - logs) * steps, 0.0)
    skip = jnp.broadcast_to(skip_ref[...], (8, head_count))
    for first, span in head_pairs(head_count, head_dim):
        x_pair = x_ref[:, span]
        sides = []
        for head in range(first, min(first + 2, head_count)):
            gap = jnp.minimum(logs[:, head : head + 1] - as_rows[head : head + 1, :], 0.0)
            mixing = jnp.exp(gap) * gram * as_rows[head_count + head : head_count + head + 1, :]
            sides.append(dot(mixing.astype(jnp.bfloat16), x_pair))
        x_wide = x_pair.astype(jnp.float32)
        lane = lax.broadcasted_iota(jnp.int32, x_pair.shape, 1)
        out_ref[:, span] = (
            jnp.where(lane < head_dim, sides[0], sides[-1])
            + pair_lanes(skip, first, head_dim)[:1] * x_wide
        )
        weighted = (pair_lanes(weight, first, head_dim) * x_wide).astype(jnp.bfloat16)
        end_ref[:, span] = dot(b_ref[...], weighted, ((0,), (0,))).astype(end_ref.dtype)


def project_kernel(slots, order_ref, *refs):
    prompt_refs = refs[:slots]
    (local_ref, c_ref, pick_ref, inherited_ref, decay_ref, arriving_ref, tail_ref, gate_ref,
     weight_ref, down_ref, up_ref, kept_ref, sent_ref, gated, low_rank) = refs[slots:]
    models, tok_rows, inner = local_ref.shape
    head_count = decay_ref.shape[2]
    head_dim = inner // head_count
    state_dim = c_ref.shape[2]
    share = tok_rows // order_ref.shape[0]
    half = models * tok_rows // 2

    @pl.when(pl.program_id(0) == 0)
    def _():
        for model in range(models):
            c_values = c_ref[model].astype(jnp.float32)
            inherited = inherited_ref[...]
            tail = jnp.broadcast_to(tail_ref[model], (8, head_count))
            mine = dot((c_values * inherited).astype(jnp.bfloat16), arriving_ref[model])
            borrowed = jnp.zeros((tok_rows, inner), jnp.float32)
            for slot in range(0, slots, 4):
                chosen = [c_values * pick_ref[:, i : i + 1] for i in range(slot, slot + 4)]
                states = [prompt_refs[i][model] for i in range(slot, slot + 4)]
                borrowed = borrowed + dot(
                    jnp.concatenate(chosen, axis=1).astype(jnp.bfloat16),
                    jnp.concatenate(states, axis=0),
                )
            decay = decay_ref[model]
            for first, span in head_pairs(head_count, head_dim):
                log_wide = pair_lanes(decay, first, head_dim)
                log_prompt = log_wide + inherited * pair_lanes(tail, first, head_dim)[:1]
                output = (
                    local_ref[model, :, span]
                    + jnp.exp(log_wide) * mine[:, span]
                    + jnp.exp(log_prompt) * borrowed[:, span]
                )
                gate = gate_ref[model, :, span].astype(jnp.float32)
                output = (output * gate / (1.0 + jnp.exp(-gate))).astype(jnp.bfloat16)
                for quarter in range(tok_rows // share):
                    rows = pl.ds(pl.multiple_of(order_ref[quarter] + model * share, share), share)
                    gated[rows, span] = output[quarter * share : (quarter + 1) * share]
        low_rank[...] = dot(gated[...], down_ref[...]).astype(jnp.bfloat16)

    policy = lax.broadcasted_iota(jnp.int32, (models * tok_rows, 1), 0) % (models * share) < share
    adapter = jnp.where(policy, dot(low_rank[...], up_ref[...]), 0.0)
    terms = (dot(gated[...], weight_ref[...]) + adapter).astype(jnp.bfloat16)
    kept_ref[...] = terms[:half]
    sent_ref[...] = terms[half:]


def head_kernel(parts, limit_ref, *refs):
    row_refs = refs[:parts]
    weight_ref, target_ref, out_ref, held, logits_ref, arrived = refs[parts:]
    each = row_refs[0].shape[0]
    tiles, _, tile = held.shape
    copies = [
        pltpu.make_async_copy(
            weight_ref.at[:, pl.ds(i * tile, tile)], held.at[i], arrived.at[i]
        )
        for i in range(tiles)
    ]
    for copy in copies:
        copy.start()
    spans = [slice(part * each, (part + 1) * each) for part in range(parts)]
    for i in range(tiles):
        copies[i].wait()
        for rows, row_ref in zip(spans, row_refs):
            logits_ref[rows, i * tile : (i + 1) * tile] = dot(row_ref[...], held[i])
    for rows in spans:
        logits = logits_ref[rows, :]
        column = lax.broadcasted_iota(jnp.int32, logits.shape, 1)
        in_range = column < limit_ref[0]
        logits = jnp.where(in_range, logits, -jnp.inf)
        top = jnp.max(logits, axis=1, keepdims=True)
        sums = jnp.sum(jnp.exp(logits - top), axis=1, keepdims=True)
        hit = (target_ref[rows, :] - limit_ref[1] == column) & in_range
        target = jnp.sum(jnp.where(hit, logits, 0.0), axis=1, keepdims=True)
        lane = lax.broadcasted_iota(jnp.int32, (each, 128), 1)
        stats = jnp.where(lane == 0, top, jnp.where(lane == 1, sums, target))
        out_ref[:, rows] = jnp.transpose(stats)[:8]


def place_kernel(count, first_ref, *refs):
    whole, arrived = refs[count:]
    copies = []
    for i in range(count):
        blocks, size = refs[i].shape[:2]
        for j in range(blocks):
            rows = pl.ds(pl.multiple_of(first_ref[i * blocks + j], 16), size)
            copies.append(
                pltpu.make_async_copy(
                    refs[i].at[j], whole.at[rows, :], arrived.at[i * blocks + j]
                )
            )
    for copy in copies:
        copy.start()
    for copy in copies:
        copy.wait()


def norm_kernel(*refs):
    *term_refs, scale_ref, out_ref = refs
    hidden = sum(term[...].astype(jnp.float32) for term in term_refs)
    mean_sq = jnp.mean(hidden * hidden, axis=1, keepdims=True)
    out_ref[...] = (hidden * lax.rsqrt(mean_sq + 1e-05) * scale_ref[...]).astype(out_ref.dtype)


def split_kernel(head_ref, *out_refs):
    size = out_refs[0].shape[0]
    for cut, out_ref in enumerate(out_refs):
        out_ref[...] = head_ref[cut * size : (cut + 1) * size, :]


def cost(flops, moved, exps=0):
    return pl.CostEstimate(flops=flops, bytes_accessed=moved, transcendentals=exps)


def whole(value):
    return pl.BlockSpec(value.shape, lambda *_: (0,) * value.ndim)


def across(x, by):
    count = lax.axis_size("mp")
    return lax.ppermute(x, "mp", [(i, (i + 2 * by) % count ^ 1) for i in range(count)])


def shards(
    scored_token_targets,
    valid,
    lengths,
    owners,
    holders,
    mixer_input_x,
    mixer_gate_input,
    input_projection_b,
    output_projection_c,
    token_step_sizes,
    head_decay_rate,
    head_skip_scale,
    prompt_held_states,
    shared_output_weight,
    adapter_down_weight,
    adapter_up_weight,
    residual,
    final_norm_scale,
    vocab_head_weight,
):
    seq_count = lax.axis_size("seq")
    mp_count = lax.axis_size("mp")
    seq_index = lax.axis_index("seq")
    mp_index = lax.axis_index("mp")
    place = place_of(seq_index)
    core = mp_index % 2
    x_count = mp_count // 2
    x_index = mp_index // 2
    tok_rows = scored_token_targets.shape[0]
    models = mixer_input_x.shape[0]
    inner_local = mixer_input_x.shape[2]
    head_count = token_step_sizes.shape[2]
    state_dim = input_projection_b.shape[2]
    roll_count = lengths.shape[0]
    width = residual.shape[2]
    blocks = seq_count // (CHAIN * SIDE)
    partners = list(itertools.product(range(SIDE), range(blocks)))[1:]
    share_rows = tok_rows // mp_count

    def from_partner(side, block):
        return partner(seq_index, side, blocks - block, seq_count)

    def beside(value):
        return [to_partner(value, side, block) for side, block in partners]

    held = jnp.transpose(prompt_held_states[:, 0], (0, 3, 1, 2)).reshape(
        models, state_dim, inner_local
    )
    states = [held, turn(held, 1), turn(held, 2)]
    states.append(turn(states[2], 1))
    beside_held = beside(held)

    first_row = seq_index * tok_rows
    offsets = jnp.arange(tok_rows, dtype=jnp.int32)
    position = first_row + offsets
    starts = jnp.cumsum(lengths) - lengths
    rollout = jnp.sum((starts[None, :] <= position[:, None]).astype(jnp.int32), axis=1) - 1
    member_table = rollout[:, None] == jnp.arange(roll_count, dtype=jnp.int32)[None, :]
    start_local = jnp.sum(jnp.where(member_table, starts[None, :], 0), axis=1) - first_row
    holder_tok = jnp.sum(jnp.where(member_table, holders[None, :], 0), axis=1)
    prompt_holder = jnp.stack(
        [
            turned(source, k)
            for k in range(CHAIN)
            for source in [seq_index] + [from_partner(side, block) for side, block in partners]
        ]
    )
    last_rollout = (offsets >= start_local[-1]).astype(jnp.float32)
    local_tail = -head_decay_rate * jnp.sum(
        token_step_sizes * last_rollout[None, :, None], axis=1
    )
    next_one = [(i, i + 1) for i in range(seq_count - 1)]
    tail = lax.ppermute(local_tail, "seq", next_one)
    pick = (holder_tok[:, None] == prompt_holder[None, :]).astype(jnp.float32)
    inherited = (start_local < 0).astype(jnp.float32)
    beside_next = beside(states[1])
    mixer_x, states[1], tail, *beside_held = tied(
        mixer_input_x, states[1], tail, *beside_held
    )

    per_model = lambda *shape: pl.BlockSpec((None,) + shape, lambda m: (m,) + (0,) * len(shape))
    local_out, local_end, decay = pl.pallas_call(
        local_kernel,
        grid=(models,),
        in_specs=[
            per_model(tok_rows, inner_local),
            per_model(tok_rows, state_dim),
            per_model(tok_rows, state_dim),
            per_model(tok_rows, head_count),
            per_model(1, head_count),
            pl.BlockSpec((tok_rows, 1), lambda m: (0, 0)),
            per_model(1, head_count),
        ],
        out_specs=[
            per_model(tok_rows, inner_local),
            per_model(state_dim, inner_local),
            per_model(tok_rows, head_count),
        ],
        out_shape=[
            jax.ShapeDtypeStruct((models, tok_rows, inner_local), jnp.float32),
            jax.ShapeDtypeStruct((models, state_dim, inner_local), jnp.bfloat16),
            jax.ShapeDtypeStruct((models, tok_rows, head_count), jnp.float32),
        ],
        compiler_params=pltpu.CompilerParams(vmem_limit_bytes=32 * 2**20),
        cost_estimate=cost(10**9, 8 * 2**20, 2 * 10**6),
        name="local_tokens",
    )(
        mixer_x,
        input_projection_b,
        output_projection_c,
        token_step_sizes,
        head_decay_rate[:, None, :],
        start_local[:, None],
        head_skip_scale[:, None, :],
    )

    hops = max(1, -(-(seq_count * tok_rows // 8) // tok_rows))
    arriving = lax.ppermute(local_end, "seq", next_one)
    if hops > 1:
        through = jnp.repeat(jnp.exp(local_tail), inner_local // head_count, axis=1)
        through = through[:, None, :] * inherited[-1]
        for _ in range(hops - 1):
            moved = through * arriving.astype(jnp.float32) + local_end.astype(jnp.float32)
            arriving = lax.ppermute(moved.astype(jnp.bfloat16), "seq", next_one)
            tail = lax.ppermute(inherited[-1] * tail + local_tail, "seq", next_one)

    head_rows, vocab_local = vocab_head_weight.shape
    part = -(-vocab_local // (CHAIN * 128)) * 128
    cuts = 2 if head_rows % 32 == 0 else 1
    cut_rows = head_rows // cuts
    head = pl.pallas_call(
        split_kernel,
        grid=(CHAIN,),
        in_specs=[pl.BlockSpec((head_rows, part), lambda j: (0, j))],
        out_specs=[pl.BlockSpec((None, cut_rows, part), lambda j: (j, 0, 0))] * cuts,
        out_shape=[jax.ShapeDtypeStruct((CHAIN, cut_rows, part), vocab_head_weight.dtype)] * cuts,
        cost_estimate=cost(0, 2 * vocab_head_weight.size * 2),
        name="split_head_columns",
    )(vocab_head_weight)
    arriving, states[3], *head = tied(arriving, states[3], *head)
    came_head = [
        lax.all_to_all(head[cut], "seq", 0, 0, axis_index_groups=chain_groups())
        for cut in range(cuts)
    ]

    besides = [beside_held, beside_next, beside(states[2]), beside(states[3])]
    prompts = []
    for state, others in zip(states, besides):
        prompts += [state] + list(others)

    quarter = jnp.arange(mp_count, dtype=jnp.int32)
    order = (quarter % 2 != core) * x_count + (quarter // 2 - x_index) % x_count
    order = order.astype(jnp.int32) * (models * share_rows)
    half = models * tok_rows // 2
    tile = 512 if width % 512 == 0 else width
    resident = [
        *prompts,
        local_out,
        output_projection_c,
        pick,
        inherited[:, None],
        decay,
        arriving,
        tail[:, None, :],
        mixer_gate_input,
    ]
    kept, sent = pl.pallas_call(
        functools.partial(project_kernel, len(prompts)),
        grid=(width // tile,),
        in_specs=[pl.BlockSpec(memory_space=pltpu.SMEM)]
        + [whole(value) for value in resident]
        + [
            pl.BlockSpec((inner_local, tile), lambda j: (0, j)),
            whole(adapter_down_weight),
            pl.BlockSpec((adapter_up_weight.shape[0], tile), lambda j: (0, j)),
        ],
        out_specs=[pl.BlockSpec((half, tile), lambda j: (0, j))] * 2,
        out_shape=[jax.ShapeDtypeStruct((half, width), jnp.bfloat16)] * 2,
        scratch_shapes=[
            pltpu.VMEM((models * tok_rows, inner_local), jnp.bfloat16),
            pltpu.VMEM((models * tok_rows, adapter_up_weight.shape[0]), jnp.bfloat16),
        ],
        compiler_params=pltpu.CompilerParams(vmem_limit_bytes=56 * 2**20),
        cost_estimate=cost(
            2 * models * tok_rows * inner_local * width, 4 * inner_local * width, 2 * 10**6
        ),
        name="gate_and_project",
    )(order, *resident, shared_output_weight, adapter_down_weight, adapter_up_weight)

    own_words = jnp.stack([scored_token_targets, valid])
    sent, came_head[0], own_words = tied(sent, came_head[0], own_words)
    words_and_valid = [own_words] + [turn(own_words, k) for k in range(1, CHAIN)]
    came = other_core(sent)
    each = models * share_rows

    def chip_sum(by):
        rows = slice(by * each, (by + 1) * each)
        return kept[rows].astype(jnp.float32) + came[rows].astype(jnp.float32)

    own_rows = lax.dynamic_slice_in_dim(residual, mp_index * share_rows, share_rows, 0)
    own_rows = jnp.transpose(own_rows, (1, 0, 2)).reshape(each, width)
    crossing = [along_x(chip_sum(by).astype(jnp.bfloat16), by) for by in range(1, x_count)]
    besides_head = [beside(came_head[0])]
    crossing[0], own_rows, came_head[-1], *came_small = tied(
        crossing[0], own_rows, came_head[-1], *words_and_valid, *besides_head[0]
    )
    words_and_valid, besides_head[0] = jnp.stack(came_small[:CHAIN]), came_small[CHAIN:]
    besides_head += [beside(piece) for piece in came_head[1:]]
    half_block = pl.BlockSpec((each, width), lambda i: (0, 0))
    normed_own = pl.pallas_call(
        norm_kernel,
        grid=(1,),
        in_specs=[half_block] * (3 + len(crossing)) + [pl.BlockSpec((1, width), lambda i: (0, 0))],
        out_specs=half_block,
        out_shape=jax.ShapeDtypeStruct((each, width), jnp.bfloat16),
        compiler_params=pltpu.CompilerParams(vmem_limit_bytes=32 * 2**20),
        cost_estimate=cost(0, 10 * each * width),
        name="add_and_norm",
    )(own_rows, kept, came, *crossing, final_norm_scale[None, :])

    limit = jnp.stack(
        [
            jnp.minimum(vocab_local - place * part, part),
            mp_index * vocab_local + place * part,
        ]
    ).astype(jnp.int32)
    mp_order = jnp.stack(
        [(x_index - k) % x_count * 2 + (core + other) % 2 for other in (0, 1) for k in range(x_count)]
    )

    def words_of(targets):
        targets = targets.reshape(CHAIN, mp_count, 1, share_rows)[:, mp_order]
        targets = jnp.broadcast_to(targets, (CHAIN, mp_count, models, share_rows))
        return targets.reshape(CHAIN, 2, x_count, each)

    tiles = 2 if part % 256 == 0 else 1

    def place_head():
        pieces, firsts = [], []
        for cut, others in enumerate(besides_head):
            pieces += [came_head[cut]] + others
            for source in [seq_index] + [from_partner(side, block) for side, block in partners]:
                first_of_chain = source - place_of(source) * SIDE
                firsts += [
                    (first_of_chain + k * SIDE) * head_rows + cut * cut_rows for k in range(CHAIN)
                ]
        return pl.pallas_call(
            functools.partial(place_kernel, len(pieces)),
            in_specs=[pl.BlockSpec(memory_space=pltpu.SMEM)]
            + [pl.BlockSpec(memory_space=pl.ANY)] * len(pieces),
            out_specs=pl.BlockSpec(memory_space=pltpu.VMEM),
            out_shape=jax.ShapeDtypeStruct((seq_count * head_rows, part), vocab_head_weight.dtype),
            scratch_shapes=[pltpu.SemaphoreType.DMA((len(pieces) * CHAIN,))],
            compiler_params=pltpu.CompilerParams(vmem_limit_bytes=16 * 2**20),
            cost_estimate=cost(0, 4 * seq_count * head_rows * part),
            name="place_head_rows",
        )(jnp.stack(firsts).astype(jnp.int32), *pieces)

    def head_stats(head_part, rows, words):
        count = len(rows)
        words = words.reshape(count * each, 1)
        stats_shape = jax.ShapeDtypeStruct((8, count * each), jnp.float32)
        return pl.pallas_call(
            functools.partial(head_kernel, count),
            in_specs=[pl.BlockSpec(memory_space=pltpu.SMEM)]
            + [pl.BlockSpec(memory_space=pltpu.VMEM)] * count
            + [pl.BlockSpec(memory_space=pl.ANY), pl.BlockSpec(memory_space=pltpu.VMEM)],
            out_specs=pl.BlockSpec(memory_space=pltpu.VMEM),
            out_shape=stats_shape,
            scratch_shapes=[
                pltpu.VMEM((tiles, width, part // tiles), jnp.bfloat16),
                pltpu.VMEM((count * each, part), jnp.float32),
                pltpu.SemaphoreType.DMA((tiles,)),
            ],
            compiler_params=pltpu.CompilerParams(vmem_limit_bytes=56 * 2**20),
            cost_estimate=cost(
                2 * count * each * width * part,
                2 * (count * each + part) * width,
                count * each * part,
            ),
            name="head_stats",
        )(limit, *rows, head_part, words).reshape(8, count, models, share_rows)

    def both_cores(values):
        return values + [other_core(value) for value in values]

    def crossed(rows):
        return [along_x(rows, by) for by in range(1, x_count)]

    blocks_of = [normed_own]
    nears = [crossed(normed_own)]
    words = words_of(words_and_valid[:, 0])
    at_end = (place == 0) | (place == CHAIN - 1)
    for step in range(1, CHAIN):
        if step == 1:
            moved = [turn(normed_own, 1), between(normed_own, [(1, 2), (2, 1)])]
        elif step == 2:
            moved = [between(inner, [(1, 0), (2, 3)]), between(blocks_of[1], [(1, 2), (2, 1)])]
        else:
            moved = [between(passed, [(1, 0), (2, 3)])]
        count = len(nears[-1])
        extra = []
        if step == CHAIN - 2:
            extra = besides_head[-1]
        elif step == CHAIN - 1:
            head_part = place_head()
            rows = [both_cores([blocks_of[k]] + nears[k]) for k in (0, 1)]
            extra = [head_stats(head_part, rows[0] + rows[1], words[:2])]
        came = tied(*nears[-1], *extra, *moved)
        nears[-1], extra, moved = came[:count], came[count : -len(moved)], came[-len(moved) :]
        if step == CHAIN - 2:
            besides_head[-1] = extra
        elif step == CHAIN - 1:
            early = extra[0]
        if step == 1:
            block, inner = moved
        elif step == 2:
            passed = moved[1]
            block = jnp.where(at_end, moved[0], passed)
        else:
            block = jnp.where(at_end, moved[0], inner)
        blocks_of.append(block)
        nears.append(crossed(block))

    last = CHAIN - 1
    middle = head_stats(
        head_part,
        both_cores([blocks_of[last - 1]] + nears[last - 1]) + both_cores([blocks_of[last]]),
        jnp.concatenate([words[last - 1].reshape(-1, each), words[last, :, 0]]),
    )
    def blocks(stats):
        return stats[:3].reshape(3, -1, 2, x_count, models, share_rows)

    first = blocks(early)
    firsts = [first] + [turn(first, by) for by in range(1, CHAIN)]
    came = tied(*nears[last], middle, *firsts)
    nears[last], middle, firsts = came[: -CHAIN - 1], came[-CHAIN - 1], came[-CHAIN:]
    rest = head_stats(head_part, both_cores(nears[last]), words[last, :, 1:])
    own_side = middle[:3, mp_count:].reshape(3, 1, 2, 1, models, share_rows)
    other_side = rest[:3].reshape(3, 1, 2, x_count - 1, models, share_rows)
    late = jnp.concatenate(
        [blocks(middle[:, :mp_count]), jnp.concatenate([own_side, other_side], axis=3)], axis=1
    )

    def merged(several):
        top = functools.reduce(jnp.maximum, [stats[0] for stats in several])
        total = sum(stats[1] * jnp.exp(stats[0] - top) for stats in several)
        return jnp.stack([top, total, sum(stats[2] for stats in several)])

    several = [jnp.concatenate([firsts[0], late], axis=1)]
    for by in range(1, CHAIN):
        stats = jnp.concatenate([firsts[by], turn(late, by)], axis=1)
        several.append(jnp.stack([stats[:, k ^ by] for k in range(CHAIN)], axis=1))
    stats = merged(several)
    several = [stats, other_core(stats)[:, :, ::-1]]
    for by in range(1, x_count):
        several.append(jnp.roll(along_x(stats, by), by, axis=3))
        several.append(jnp.roll(across(stats, by)[:, :, ::-1], by, axis=3))
    stats = merged(several)
    logprob = stats[2] - stats[0] - jnp.log(stats[1])
    delta = (logprob[:, :, :, 0] - logprob[:, :, :, 1]).reshape(CHAIN, mp_count, share_rows)
    in_order = mp_order[None, :] == quarter[:, None]
    delta = jnp.sum(jnp.where(in_order[None, :, :, None], delta[:, None], 0.0), axis=2)
    delta = delta.reshape(CHAIN, tok_rows) * words_and_valid[:, 1].astype(jnp.float32)
    token_delta = delta[0]
    first_rows = jnp.stack([turned(seq_index, k) for k in range(CHAIN)]) * tok_rows
    since = (first_rows[:, None] + offsets[None, :])[:, :, None] - starts
    member = ((since >= 0) & (since < lengths)).astype(jnp.float32)
    roll_sums = jnp.dot(
        delta.reshape(-1), member.reshape(-1, roll_count), precision=highest
    )
    roll_sums = roll_sums + sum(beside(roll_sums))
    owner_sums = jnp.where(owners == seq_index, roll_sums / lengths.astype(jnp.float32), 0.0)
    return (owner_sums[None, :], token_delta)


def solution(mesh):
    placed = (
        P("seq"),
        P("seq"),
        P(),
        P(),
        P(),
        P(None, "seq", "mp"),
        P(None, "seq", "mp"),
        P(None, "seq", None),
        P(None, "seq", None),
        P(None, "seq", "mp"),
        P(None, "mp"),
        P(None, "mp"),
        P(None, "seq", "mp", None, None),
        P("mp", None),
        P("mp", None),
        P(),
        P("seq", None, None),
        P(),
        P("seq", "mp"),
    )
    return jax.shard_map(
        shards, mesh=mesh, in_specs=placed, out_specs=(P("seq", None), P("seq")), check_vma=False
    )
```

```python
import functools
import itertools

import jax
import jax.numpy as jnp
from jax import lax
from jax.experimental import pallas as pl
from jax.experimental.pallas import tpu as pltpu
from jax.sharding import PartitionSpec as P

highest = lax.Precision.HIGHEST
CHAIN = 4
TAIL_ROWS = 16
SIDE = 2


def place_of(i):
    return (i // SIDE) % CHAIN


def turned(i, by):
    return i ^ (by * SIDE)


def partner(i, side, block, count):
    return ((i ^ side) + block * CHAIN * SIDE) % count


def turn(x, by):
    count = lax.axis_size("seq")
    return lax.ppermute(x, "seq", [(i, turned(i, by)) for i in range(count)])


def to_partner(x, side, block):
    count = lax.axis_size("seq")
    return lax.ppermute(x, "seq", [(i, partner(i, side, block, count)) for i in range(count)])


def between(x, pairs):
    count = lax.axis_size("seq")
    sends = [
        (i, i + (to - place) * SIDE)
        for i in range(count)
        for place, to in pairs
        if place_of(i) == place
    ]
    return lax.ppermute(x, "seq", sends)


def chain_groups():
    count = lax.axis_size("seq")
    return [
        [first + k * SIDE for k in range(CHAIN)] for first in range(count) if place_of(first) == 0
    ]


def other_core(x):
    count = lax.axis_size("mp")
    return lax.ppermute(x, "mp", [(i, i ^ 1) for i in range(count)])


def along_x(x, by):
    count = lax.axis_size("mp")
    return lax.ppermute(x, "mp", [(i, (i + 2 * by) % count) for i in range(count)])


def tied(*values):
    return list(lax.optimization_barrier(values))


def dot(a, b, over=((1,), (0,))):
    return lax.dot_general(a, b, (over, ((), ())), preferred_element_type=jnp.float32)


def exact(a, b):
    return lax.dot_general(
        a, b, (((1,), (0,)), ((), ())), precision=highest, preferred_element_type=jnp.float32
    )


def head_pairs(head_count, head_dim):
    return [
        (first, slice(first * head_dim, min(first + 2, head_count) * head_dim))
        for first in range(0, head_count, 2)
    ]


def pair_lanes(values, first, head_dim):
    if first + 1 == values.shape[1]:
        return jnp.broadcast_to(values[:, first : first + 1], (values.shape[0], head_dim))
    lane = lax.broadcasted_iota(jnp.int32, (values.shape[0], 2 * head_dim), 1)
    return jnp.where(lane < head_dim, values[:, first : first + 1], values[:, first + 1 : first + 2])


def local_kernel(
    x_ref, both_ref, step_ref, rate_ref, start_ref, skip_ref, out_ref, end_ref, decay_ref,
):
    tok_rows, inner = x_ref.shape
    head_count = step_ref.shape[1]
    head_dim = inner // head_count
    state_dim = both_ref.shape[1] // 2
    b_values, c_values = both_ref[:, :state_dim], both_ref[:, state_dim:]
    row = lax.broadcasted_iota(jnp.int32, (tok_rows, tok_rows), 0)
    col = lax.broadcasted_iota(jnp.int32, (tok_rows, tok_rows), 1)
    causal = (col >= start_ref[...]) & (col <= row)
    gram = jnp.where(causal, dot(c_values, b_values, ((1,), (1,))), 0.0)
    steps = step_ref[...]
    logs = exact(jnp.where(col <= row, 1.0, 0.0), -steps * rate_ref[...])
    decay = logs - exact(jnp.where(col == start_ref[...] - 1, 1.0, 0.0), logs)
    decay_ref[...] = decay
    since = jnp.broadcast_to(decay[tok_rows - 1 :, :], (TAIL_ROWS, head_count))
    term = lax.broadcasted_iota(jnp.int32, since.shape, 0)
    high = since.astype(jnp.bfloat16).astype(jnp.float32)
    middle = (since - high).astype(jnp.bfloat16).astype(jnp.float32)
    low = since - high - middle
    since = jnp.where(term == 0, high, jnp.where(term == 1, middle, jnp.where(term == 2, low, 0.0)))
    fill = jnp.zeros((tok_rows, 128 - 2 * head_count), jnp.float32)
    as_rows = jnp.transpose(jnp.concatenate([logs, steps, fill], axis=1))
    last_log = logs[tok_rows - 1 :, :]
    last_start = start_ref[tok_rows - 1 :, :]
    place = lax.broadcasted_iota(jnp.int32, (tok_rows, 1), 0)
    weight = jnp.where(place >= last_start, jnp.exp(last_log - logs) * steps, 0.0)
    skip = jnp.broadcast_to(skip_ref[...], (8, head_count))
    for first, span in head_pairs(head_count, head_dim):
        x_pair = x_ref[:, span]
        sides = []
        for head in range(first, min(first + 2, head_count)):
            gap = jnp.minimum(logs[:, head : head + 1] - as_rows[head : head + 1, :], 0.0)
            mixing = jnp.exp(gap) * gram * as_rows[head_count + head : head_count + head + 1, :]
            sides.append(dot(mixing.astype(jnp.bfloat16), x_pair))
        x_wide = x_pair.astype(jnp.float32)
        lane = lax.broadcasted_iota(jnp.int32, x_pair.shape, 1)
        out_ref[:, span] = (
            jnp.where(lane < head_dim, sides[0], sides[-1])
            + pair_lanes(skip, first, head_dim)[:1] * x_wide
        )
        tail = pair_lanes(since, first, head_dim)
        end_ref[state_dim:, span] = tail.astype(end_ref.dtype)
        weighted = (pair_lanes(weight, first, head_dim) * x_wide).astype(jnp.bfloat16)
        end_ref[:state_dim, span] = dot(b_values, weighted, ((0,), (0,))).astype(end_ref.dtype)


def project_kernel(slots, joined, order_ref, *refs):
    prompt_refs = refs[:slots]
    (local_ref, both_ref, pick_ref, inherited_ref, decay_ref, arriving_ref, tail_ref, gate_ref,
     weight_ref, down_ref, up_ref, kept_ref, sent_ref, gated, low_rank) = refs[slots:]
    models, tok_rows, inner = local_ref.shape
    head_count = decay_ref.shape[2]
    head_dim = inner // head_count
    state_dim = both_ref.shape[2] // 2
    share = tok_rows // order_ref.shape[0]
    half = models * tok_rows // 2

    @pl.when(pl.program_id(0) == 0)
    def _():
        for model in range(models):
            c_values = both_ref[model][:, state_dim:].astype(jnp.float32)
            inherited = inherited_ref[...]
            mine = dot(
                (c_values * inherited).astype(jnp.bfloat16), arriving_ref[model, :state_dim, :]
            )
            tail = jnp.broadcast_to(tail_ref[model], (8, head_count))
            sent_tail = arriving_ref[model, state_dim:, :].astype(jnp.float32)
            sent_tail = jnp.sum(sent_tail, axis=0, keepdims=True)
            borrowed = jnp.zeros((tok_rows, inner), jnp.float32)
            for slot in range(0, slots, 4):
                chosen = [c_values * pick_ref[:, i : i + 1] for i in range(slot, slot + 4)]
                states = [prompt_refs[i][model] for i in range(slot, slot + 4)]
                borrowed = borrowed + dot(
                    jnp.concatenate(chosen, axis=1).astype(jnp.bfloat16),
                    jnp.concatenate(states, axis=0),
                )
            decay = decay_ref[model]
            for first, span in head_pairs(head_count, head_dim):
                log_wide = pair_lanes(decay, first, head_dim)
                since = sent_tail[:, span] if joined else pair_lanes(tail, first, head_dim)[:1]
                log_prompt = log_wide + inherited * since
                output = (
                    local_ref[model, :, span]
                    + jnp.exp(log_wide) * mine[:, span]
                    + jnp.exp(log_prompt) * borrowed[:, span]
                )
                gate = gate_ref[model, :, span].astype(jnp.float32)
                output = (output * gate / (1.0 + jnp.exp(-gate))).astype(jnp.bfloat16)
                for quarter in range(tok_rows // share):
                    rows = pl.ds(pl.multiple_of(order_ref[quarter] + model * share, share), share)
                    gated[rows, span] = output[quarter * share : (quarter + 1) * share]
        low_rank[...] = dot(gated[...], down_ref[...]).astype(jnp.bfloat16)

    policy = lax.broadcasted_iota(jnp.int32, (models * tok_rows, 1), 0) % (models * share) < share
    adapter = jnp.where(policy, dot(low_rank[...], up_ref[...]), 0.0)
    terms = (dot(gated[...], weight_ref[...]) + adapter).astype(jnp.bfloat16)
    kept_ref[...] = terms[:half]
    sent_ref[...] = terms[half:]


def head_kernel(parts, limit_ref, *refs):
    row_refs = refs[:parts]
    weight_ref, target_ref, out_ref, held, logits_ref, arrived = refs[parts:]
    each = row_refs[0].shape[0]
    tiles, _, tile = held.shape
    copies = [
        pltpu.make_async_copy(
            weight_ref.at[:, pl.ds(i * tile, tile)], held.at[i], arrived.at[i]
        )
        for i in range(tiles)
    ]
    for copy in copies:
        copy.start()
    spans = [slice(part * each, (part + 1) * each) for part in range(parts)]
    for i in range(tiles):
        copies[i].wait()
        for rows, row_ref in zip(spans, row_refs):
            logits_ref[rows, i * tile : (i + 1) * tile] = dot(row_ref[...], held[i])
    for rows in spans:
        logits = logits_ref[rows, :]
        column = lax.broadcasted_iota(jnp.int32, logits.shape, 1)
        in_range = column < limit_ref[0]
        logits = jnp.where(in_range, logits, -jnp.inf)
        top = jnp.max(logits, axis=1, keepdims=True)
        sums = jnp.sum(jnp.exp(logits - top), axis=1, keepdims=True)
        hit = (target_ref[rows, :] - limit_ref[1] == column) & in_range
        target = jnp.sum(jnp.where(hit, logits, 0.0), axis=1, keepdims=True)
        lane = lax.broadcasted_iota(jnp.int32, (each, 128), 1)
        stats = jnp.where(lane == 0, top, jnp.where(lane == 1, sums, target))
        out_ref[:, rows] = jnp.transpose(stats)[:8]


def place_kernel(count, first_ref, *refs):
    whole, arrived = refs[count:]
    copies = []
    for i in range(count):
        blocks, size = refs[i].shape[:2]
        for j in range(blocks):
            rows = pl.ds(pl.multiple_of(first_ref[i * blocks + j], 16), size)
            copies.append(
                pltpu.make_async_copy(
                    refs[i].at[j], whole.at[rows, :], arrived.at[i * blocks + j]
                )
            )
    for copy in copies:
        copy.start()
    for copy in copies:
        copy.wait()


def norm_kernel(*refs):
    *term_refs, scale_ref, out_ref = refs
    hidden = sum(term[...].astype(jnp.float32) for term in term_refs)
    mean_sq = jnp.mean(hidden * hidden, axis=1, keepdims=True)
    out_ref[...] = (hidden * lax.rsqrt(mean_sq + 1e-05) * scale_ref[...]).astype(out_ref.dtype)


def split_kernel(head_ref, *out_refs):
    size = out_refs[0].shape[0]
    for cut, out_ref in enumerate(out_refs):
        out_ref[...] = head_ref[cut * size : (cut + 1) * size, :]


def cost(flops, moved, exps=0):
    return pl.CostEstimate(flops=flops, bytes_accessed=moved, transcendentals=exps)


def whole(value):
    return pl.BlockSpec(value.shape, lambda *_: (0,) * value.ndim)


def across(x, by):
    count = lax.axis_size("mp")
    return lax.ppermute(x, "mp", [(i, (i + 2 * by) % count ^ 1) for i in range(count)])


def shards(
    scored_token_targets,
    valid,
    lengths,
    owners,
    holders,
    mixer_input_x,
    mixer_gate_input,
    input_projection_b,
    output_projection_c,
    token_step_sizes,
    head_decay_rate,
    head_skip_scale,
    prompt_held_states,
    shared_output_weight,
    adapter_down_weight,
    adapter_up_weight,
    residual,
    final_norm_scale,
    vocab_head_weight,
):
    seq_count = lax.axis_size("seq")
    mp_count = lax.axis_size("mp")
    seq_index = lax.axis_index("seq")
    mp_index = lax.axis_index("mp")
    place = place_of(seq_index)
    core = mp_index % 2
    x_count = mp_count // 2
    x_index = mp_index // 2
    tok_rows = scored_token_targets.shape[0]
    models = mixer_input_x.shape[0]
    inner_local = mixer_input_x.shape[2]
    head_count = token_step_sizes.shape[2]
    state_dim = input_projection_b.shape[2]
    roll_count = lengths.shape[0]
    width = residual.shape[2]
    blocks = seq_count // (CHAIN * SIDE)
    partners = list(itertools.product(range(SIDE), range(blocks)))[1:]
    share_rows = tok_rows // mp_count

    def from_partner(side, block):
        return partner(seq_index, side, blocks - block, seq_count)

    def beside(value):
        return [to_partner(value, side, block) for side, block in partners]

    held = jnp.transpose(prompt_held_states[:, 0], (0, 3, 1, 2)).reshape(
        models, state_dim, inner_local
    )
    states = [held, turn(held, 1), turn(held, 2)]
    states.append(turn(states[2], 1))
    beside_held = beside(held)

    first_row = seq_index * tok_rows
    offsets = jnp.arange(tok_rows, dtype=jnp.int32)
    position = first_row + offsets
    starts = jnp.cumsum(lengths) - lengths
    rollout = jnp.sum((starts[None, :] <= position[:, None]).astype(jnp.int32), axis=1) - 1
    member_table = rollout[:, None] == jnp.arange(roll_count, dtype=jnp.int32)[None, :]
    start_local = jnp.sum(jnp.where(member_table, starts[None, :], 0), axis=1) - first_row
    holder_tok = jnp.sum(jnp.where(member_table, holders[None, :], 0), axis=1)
    prompt_holder = jnp.stack(
        [
            turned(source, k)
            for k in range(CHAIN)
            for source in [seq_index] + [from_partner(side, block) for side, block in partners]
        ]
    )
    both_projections = jnp.concatenate([input_projection_b, output_projection_c], axis=2)
    pick = (holder_tok[:, None] == prompt_holder[None, :]).astype(jnp.float32)
    inherited = (start_local < 0).astype(jnp.float32)
    beside_next = beside(states[1])
    mixer_x, states[1], *beside_held = tied(mixer_input_x, states[1], *beside_held)

    per_model = lambda *shape: pl.BlockSpec((None,) + shape, lambda m: (m,) + (0,) * len(shape))
    local_out, local_end, decay = pl.pallas_call(
        local_kernel,
        grid=(models,),
        in_specs=[
            per_model(tok_rows, inner_local),
            per_model(tok_rows, 2 * state_dim),
            per_model(tok_rows, head_count),
            per_model(1, head_count),
            pl.BlockSpec((tok_rows, 1), lambda m: (0, 0)),
            per_model(1, head_count),
        ],
        out_specs=[
            per_model(tok_rows, inner_local),
            per_model(state_dim + TAIL_ROWS, inner_local),
            per_model(tok_rows, head_count),
        ],
        out_shape=[
            jax.ShapeDtypeStruct((models, tok_rows, inner_local), jnp.float32),
            jax.ShapeDtypeStruct((models, state_dim + TAIL_ROWS, inner_local), jnp.bfloat16),
            jax.ShapeDtypeStruct((models, tok_rows, head_count), jnp.float32),
        ],
        compiler_params=pltpu.CompilerParams(vmem_limit_bytes=32 * 2**20),
        cost_estimate=cost(10**9, 8 * 2**20, 2 * 10**6),
        name="local_tokens",
    )(
        mixer_x,
        both_projections,
        token_step_sizes,
        head_decay_rate[:, None, :],
        start_local[:, None],
        head_skip_scale[:, None, :],
    )

    hops = max(1, -(-(seq_count * tok_rows // 8) // tok_rows))
    next_one = [(i, i + 1) for i in range(seq_count - 1)]
    arriving = lax.ppermute(local_end, "seq", next_one)
    tail = jnp.zeros((models, head_count), jnp.float32)
    if hops > 1:
        local_tail = decay[:, -1]
        tail = lax.ppermute(local_tail, "seq", next_one)
        through = jnp.repeat(jnp.exp(local_tail), inner_local // head_count, axis=1)
        through = through[:, None, :] * inherited[-1]
        for _ in range(hops - 1):
            moved = through * arriving.astype(jnp.float32) + local_end.astype(jnp.float32)
            arriving = lax.ppermute(moved.astype(jnp.bfloat16), "seq", next_one)
            tail = lax.ppermute(inherited[-1] * tail + local_tail, "seq", next_one)

    head_rows, vocab_local = vocab_head_weight.shape
    part = -(-vocab_local // (CHAIN * 128)) * 128
    cuts = 2 if head_rows % 32 == 0 else 1
    cut_rows = head_rows // cuts
    head = pl.pallas_call(
        split_kernel,
        grid=(CHAIN,),
        in_specs=[pl.BlockSpec((head_rows, part), lambda j: (0, j))],
        out_specs=[pl.BlockSpec((None, cut_rows, part), lambda j: (j, 0, 0))] * cuts,
        out_shape=[jax.ShapeDtypeStruct((CHAIN, cut_rows, part), vocab_head_weight.dtype)] * cuts,
        cost_estimate=cost(0, 2 * vocab_head_weight.size * 2),
        name="split_head_columns",
    )(vocab_head_weight)
    arriving, states[3], *head = tied(arriving, states[3], *head)
    came_head = [
        lax.all_to_all(head[cut], "seq", 0, 0, axis_index_groups=chain_groups())
        for cut in range(cuts)
    ]

    besides = [beside_held, beside_next, beside(states[2]), beside(states[3])]
    prompts = []
    for state, others in zip(states, besides):
        prompts += [state] + list(others)

    quarter = jnp.arange(mp_count, dtype=jnp.int32)
    order = (quarter % 2 != core) * x_count + (quarter // 2 - x_index) % x_count
    order = order.astype(jnp.int32) * (models * share_rows)
    half = models * tok_rows // 2
    tile = 512 if width % 512 == 0 else width
    resident = [
        *prompts,
        local_out,
        both_projections,
        pick,
        inherited[:, None],
        decay,
        arriving,
        tail[:, None, :],
        mixer_gate_input,
    ]
    kept, sent = pl.pallas_call(
        functools.partial(project_kernel, len(prompts), hops == 1),
        grid=(width // tile,),
        in_specs=[pl.BlockSpec(memory_space=pltpu.SMEM)]
        + [whole(value) for value in resident]
        + [
            pl.BlockSpec((inner_local, tile), lambda j: (0, j)),
            whole(adapter_down_weight),
            pl.BlockSpec((adapter_up_weight.shape[0], tile), lambda j: (0, j)),
        ],
        out_specs=[pl.BlockSpec((half, tile), lambda j: (0, j))] * 2,
        out_shape=[jax.ShapeDtypeStruct((half, width), jnp.bfloat16)] * 2,
        scratch_shapes=[
            pltpu.VMEM((models * tok_rows, inner_local), jnp.bfloat16),
            pltpu.VMEM((models * tok_rows, adapter_up_weight.shape[0]), jnp.bfloat16),
        ],
        compiler_params=pltpu.CompilerParams(vmem_limit_bytes=56 * 2**20),
        cost_estimate=cost(
            2 * models * tok_rows * inner_local * width, 4 * inner_local * width, 2 * 10**6
        ),
        name="gate_and_project",
    )(order, *resident, shared_output_weight, adapter_down_weight, adapter_up_weight)

    own_words = jnp.stack([scored_token_targets, valid])
    sent, came_head[0], own_words = tied(sent, came_head[0], own_words)
    words_and_valid = [own_words] + [turn(own_words, k) for k in range(1, CHAIN)]
    came = other_core(sent)
    each = models * share_rows

    def chip_sum(by):
        rows = slice(by * each, (by + 1) * each)
        return kept[rows].astype(jnp.float32) + came[rows].astype(jnp.float32)

    own_rows = lax.dynamic_slice_in_dim(residual, mp_index * share_rows, share_rows, 0)
    own_rows = jnp.transpose(own_rows, (1, 0, 2)).reshape(each, width)
    crossing = [along_x(chip_sum(by).astype(jnp.bfloat16), by) for by in range(1, x_count)]
    besides_head = [beside(came_head[0])]
    crossing[0], own_rows, came_head[-1], *words_and_valid = tied(
        crossing[0], own_rows, came_head[-1], *words_and_valid
    )
    words_and_valid = jnp.stack(words_and_valid)
    besides_head += [beside(piece) for piece in came_head[1:]]
    half_block = pl.BlockSpec((each, width), lambda i: (0, 0))
    normed_own = pl.pallas_call(
        norm_kernel,
        grid=(1,),
        in_specs=[half_block] * (3 + len(crossing)) + [pl.BlockSpec((1, width), lambda i: (0, 0))],
        out_specs=half_block,
        out_shape=jax.ShapeDtypeStruct((each, width), jnp.bfloat16),
        compiler_params=pltpu.CompilerParams(vmem_limit_bytes=32 * 2**20),
        cost_estimate=cost(0, 10 * each * width),
        name="add_and_norm",
    )(own_rows, kept, came, *crossing, final_norm_scale[None, :])
    normed_own, *besides_head[0] = tied(normed_own, *besides_head[0])

    limit = jnp.stack(
        [
            jnp.minimum(vocab_local - place * part, part),
            mp_index * vocab_local + place * part,
        ]
    ).astype(jnp.int32)
    mp_order = jnp.stack(
        [(x_index - k) % x_count * 2 + (core + other) % 2 for other in (0, 1) for k in range(x_count)]
    )

    def words_of(targets):
        targets = targets.reshape(CHAIN, mp_count, 1, share_rows)[:, mp_order]
        targets = jnp.broadcast_to(targets, (CHAIN, mp_count, models, share_rows))
        return targets.reshape(CHAIN, 2, x_count, each)

    tiles = 2 if part % 256 == 0 else 1

    def place_head():
        pieces, firsts = [], []
        for cut, others in enumerate(besides_head):
            pieces += [came_head[cut]] + others
            for source in [seq_index] + [from_partner(side, block) for side, block in partners]:
                first_of_chain = source - place_of(source) * SIDE
                firsts += [
                    (first_of_chain + k * SIDE) * head_rows + cut * cut_rows for k in range(CHAIN)
                ]
        return pl.pallas_call(
            functools.partial(place_kernel, len(pieces)),
            in_specs=[pl.BlockSpec(memory_space=pltpu.SMEM)]
            + [pl.BlockSpec(memory_space=pl.ANY)] * len(pieces),
            out_specs=pl.BlockSpec(memory_space=pltpu.VMEM),
            out_shape=jax.ShapeDtypeStruct((seq_count * head_rows, part), vocab_head_weight.dtype),
            scratch_shapes=[pltpu.SemaphoreType.DMA((len(pieces) * CHAIN,))],
            compiler_params=pltpu.CompilerParams(vmem_limit_bytes=16 * 2**20),
            cost_estimate=cost(0, 4 * seq_count * head_rows * part),
            name="place_head_rows",
        )(jnp.stack(firsts).astype(jnp.int32), *pieces)

    def head_stats(head_part, rows, words):
        count = len(rows)
        words = words.reshape(count * each, 1)
        stats_shape = jax.ShapeDtypeStruct((8, count * each), jnp.float32)
        return pl.pallas_call(
            functools.partial(head_kernel, count),
            in_specs=[pl.BlockSpec(memory_space=pltpu.SMEM)]
            + [pl.BlockSpec(memory_space=pltpu.VMEM)] * count
            + [pl.BlockSpec(memory_space=pl.ANY), pl.BlockSpec(memory_space=pltpu.VMEM)],
            out_specs=pl.BlockSpec(memory_space=pltpu.VMEM),
            out_shape=stats_shape,
            scratch_shapes=[
                pltpu.VMEM((tiles, width, part // tiles), jnp.bfloat16),
                pltpu.VMEM((count * each, part), jnp.float32),
                pltpu.SemaphoreType.DMA((tiles,)),
            ],
            compiler_params=pltpu.CompilerParams(vmem_limit_bytes=56 * 2**20),
            cost_estimate=cost(
                2 * count * each * width * part,
                2 * (count * each + part) * width,
                count * each * part,
            ),
            name="head_stats",
        )(limit, *rows, head_part, words).reshape(8, count, models, share_rows)

    def both_cores(values):
        return values + [other_core(value) for value in values]

    def crossed(rows):
        return [along_x(rows, by) for by in range(1, x_count)]

    blocks_of = [normed_own]
    nears = [crossed(normed_own)]
    words = words_of(words_and_valid[:, 0])
    at_end = (place == 0) | (place == CHAIN - 1)
    for step in range(1, CHAIN):
        if step == 1:
            moved = [turn(normed_own, 1), between(normed_own, [(1, 2), (2, 1)])]
        elif step == 2:
            moved = [between(inner, [(1, 0), (2, 3)]), between(blocks_of[1], [(1, 2), (2, 1)])]
        else:
            moved = [between(passed, [(1, 0), (2, 3)])]
        count = len(nears[-1])
        extra = []
        if step == CHAIN - 2:
            extra = besides_head[-1]
        elif step == CHAIN - 1:
            head_part = place_head()
            rows = both_cores([blocks_of[0]] + nears[0])
            extra = [head_stats(head_part, rows, words[0])]
        came = tied(*nears[-1], *extra, *moved)
        nears[-1], extra, moved = came[:count], came[count : -len(moved)], came[-len(moved) :]
        if step == CHAIN - 2:
            besides_head[-1] = extra
        elif step == CHAIN - 1:
            early = extra[0]
        if step == 1:
            block, inner = moved
        elif step == 2:
            passed = moved[1]
            block = jnp.where(at_end, moved[0], passed)
        else:
            block = jnp.where(at_end, moved[0], inner)
        blocks_of.append(block)
        nears.append(crossed(block))

    last = CHAIN - 1
    rows = [both_cores([blocks_of[k]] + nears[k]) for k in range(1, last)]
    middle = head_stats(
        head_part,
        [value for values in rows for value in values] + both_cores([blocks_of[last]]),
        jnp.concatenate([words[1:last].reshape(-1, each), words[last, :, 0]]),
    )
    def blocks(stats):
        return stats[:3].reshape(3, -1, 2, x_count, models, share_rows)

    *nears[last], middle, early = tied(*nears[last], middle, early)
    rest = head_stats(head_part, both_cores(nears[last]), words[last, :, 1:])
    whole_blocks = (last - 1) * mp_count
    own_side = middle[:3, whole_blocks:].reshape(3, 1, 2, 1, models, share_rows)
    other_side = rest[:3].reshape(3, 1, 2, x_count - 1, models, share_rows)
    stats = jnp.concatenate(
        [
            blocks(early),
            blocks(middle[:, :whole_blocks]),
            jnp.concatenate([own_side, other_side], axis=3),
        ],
        axis=1,
    )

    def merged(several):
        top = functools.reduce(jnp.maximum, [stats[0] for stats in several])
        total = sum(stats[1] * jnp.exp(stats[0] - top) for stats in several)
        return jnp.stack([top, total, sum(stats[2] for stats in several)])

    several = [stats]
    for by in range(1, CHAIN):
        came = turn(stats, by)
        several.append(jnp.stack([came[:, k ^ by] for k in range(CHAIN)], axis=1))
    stats = merged(several)
    several = [stats, other_core(stats)[:, :, ::-1]]
    for by in range(1, x_count):
        several.append(jnp.roll(along_x(stats, by), by, axis=3))
        several.append(jnp.roll(across(stats, by)[:, :, ::-1], by, axis=3))
    stats = merged(several)
    logprob = stats[2] - stats[0] - jnp.log(stats[1])
    delta = (logprob[:, :, :, 0] - logprob[:, :, :, 1]).reshape(CHAIN, mp_count, share_rows)
    in_order = mp_order[None, :] == quarter[:, None]
    delta = jnp.sum(jnp.where(in_order[None, :, :, None], delta[:, None], 0.0), axis=2)
    delta = delta.reshape(CHAIN, tok_rows) * words_and_valid[:, 1].astype(jnp.float32)
    token_delta = delta[0]
    first_rows = jnp.stack([turned(seq_index, k) for k in range(CHAIN)]) * tok_rows
    since = (first_rows[:, None] + offsets[None, :])[:, :, None] - starts
    member = ((since >= 0) & (since < lengths)).astype(jnp.float32)
    roll_sums = jnp.dot(
        delta.reshape(-1), member.reshape(-1, roll_count), precision=highest
    )
    roll_sums = roll_sums + sum(beside(roll_sums))
    owner_sums = jnp.where(owners == seq_index, roll_sums / lengths.astype(jnp.float32), 0.0)
    return (owner_sums[None, :], token_delta)


def solution(mesh):
    placed = (
        P("seq"),
        P("seq"),
        P(),
        P(),
        P(),
        P(None, "seq", "mp"),
        P(None, "seq", "mp"),
        P(None, "seq", None),
        P(None, "seq", None),
        P(None, "seq", "mp"),
        P(None, "mp"),
        P(None, "mp"),
        P(None, "seq", "mp", None, None),
        P("mp", None),
        P("mp", None),
        P(),
        P("seq", None, None),
        P(),
        P("seq", "mp"),
    )
    return jax.shard_map(
        shards, mesh=mesh, in_specs=placed, out_specs=(P("seq", None), P("seq")), check_vma=False
    )
```

```python
import functools
import itertools

import jax
import jax.numpy as jnp
from jax import lax
from jax.experimental import pallas as pl
from jax.experimental.pallas import tpu as pltpu
from jax.sharding import PartitionSpec as P

highest = lax.Precision.HIGHEST
CHAIN = 4
TAIL_ROWS = 16
SIDE = 2


def place_of(i):
    return (i // SIDE) % CHAIN


def turned(i, by):
    return i ^ (by * SIDE)


def partner(i, side, block, count):
    return ((i ^ side) + block * CHAIN * SIDE) % count


def turn(x, by):
    count = lax.axis_size("seq")
    return lax.ppermute(x, "seq", [(i, turned(i, by)) for i in range(count)])


def to_partner(x, side, block):
    count = lax.axis_size("seq")
    return lax.ppermute(x, "seq", [(i, partner(i, side, block, count)) for i in range(count)])


def between(x, pairs):
    count = lax.axis_size("seq")
    sends = [
        (i, i + (to - place) * SIDE)
        for i in range(count)
        for place, to in pairs
        if place_of(i) == place
    ]
    return lax.ppermute(x, "seq", sends)


def chain_groups():
    count = lax.axis_size("seq")
    return [
        [first + k * SIDE for k in range(CHAIN)] for first in range(count) if place_of(first) == 0
    ]


def other_core(x):
    count = lax.axis_size("mp")
    return lax.ppermute(x, "mp", [(i, i ^ 1) for i in range(count)])


def along_x(x, by):
    count = lax.axis_size("mp")
    return lax.ppermute(x, "mp", [(i, (i + 2 * by) % count) for i in range(count)])


def tied(*values):
    return list(lax.optimization_barrier(values))


def dot(a, b, over=((1,), (0,))):
    return lax.dot_general(a, b, (over, ((), ())), preferred_element_type=jnp.float32)


def exact(a, b):
    return lax.dot_general(
        a, b, (((1,), (0,)), ((), ())), precision=highest, preferred_element_type=jnp.float32
    )


def head_pairs(head_count, head_dim):
    return [
        (first, slice(first * head_dim, min(first + 2, head_count) * head_dim))
        for first in range(0, head_count, 2)
    ]


def pair_lanes(values, first, head_dim):
    if first + 1 == values.shape[1]:
        return jnp.broadcast_to(values[:, first : first + 1], (values.shape[0], head_dim))
    lane = lax.broadcasted_iota(jnp.int32, (values.shape[0], 2 * head_dim), 1)
    return jnp.where(lane < head_dim, values[:, first : first + 1], values[:, first + 1 : first + 2])


def local_kernel(
    x_ref, both_ref, step_ref, rate_ref, start_ref, skip_ref, out_ref, end_ref, decay_ref,
):
    tok_rows, inner = x_ref.shape
    head_count = step_ref.shape[1]
    head_dim = inner // head_count
    state_dim = both_ref.shape[1] // 2
    b_values, c_values = both_ref[:, :state_dim], both_ref[:, state_dim:]
    row = lax.broadcasted_iota(jnp.int32, (tok_rows, tok_rows), 0)
    col = lax.broadcasted_iota(jnp.int32, (tok_rows, tok_rows), 1)
    causal = (col >= start_ref[...]) & (col <= row)
    gram = jnp.where(causal, dot(c_values, b_values, ((1,), (1,))), 0.0)
    steps = step_ref[...]
    logs = exact(jnp.where(col <= row, 1.0, 0.0), -steps * rate_ref[...])
    decay = logs - exact(jnp.where(col == start_ref[...] - 1, 1.0, 0.0), logs)
    decay_ref[...] = decay
    since = jnp.broadcast_to(decay[tok_rows - 1 :, :], (TAIL_ROWS, head_count))
    term = lax.broadcasted_iota(jnp.int32, since.shape, 0)
    high = since.astype(jnp.bfloat16).astype(jnp.float32)
    middle = (since - high).astype(jnp.bfloat16).astype(jnp.float32)
    low = since - high - middle
    since = jnp.where(term == 0, high, jnp.where(term == 1, middle, jnp.where(term == 2, low, 0.0)))
    fill = jnp.zeros((tok_rows, 128 - 2 * head_count), jnp.float32)
    as_rows = jnp.transpose(jnp.concatenate([logs, steps, fill], axis=1))
    last_log = logs[tok_rows - 1 :, :]
    last_start = start_ref[tok_rows - 1 :, :]
    place = lax.broadcasted_iota(jnp.int32, (tok_rows, 1), 0)
    weight = jnp.where(place >= last_start, jnp.exp(last_log - logs) * steps, 0.0)
    skip = jnp.broadcast_to(skip_ref[...], (8, head_count))
    for first, span in head_pairs(head_count, head_dim):
        x_pair = x_ref[:, span]
        sides = []
        for head in range(first, min(first + 2, head_count)):
            gap = jnp.minimum(logs[:, head : head + 1] - as_rows[head : head + 1, :], 0.0)
            mixing = jnp.exp(gap) * gram * as_rows[head_count + head : head_count + head + 1, :]
            sides.append(dot(mixing.astype(jnp.bfloat16), x_pair))
        x_wide = x_pair.astype(jnp.float32)
        lane = lax.broadcasted_iota(jnp.int32, x_pair.shape, 1)
        out_ref[:, span] = (
            jnp.where(lane < head_dim, sides[0], sides[-1])
            + pair_lanes(skip, first, head_dim)[:1] * x_wide
        )
        tail = pair_lanes(since, first, head_dim)
        end_ref[state_dim:, span] = tail.astype(end_ref.dtype)
        weighted = (pair_lanes(weight, first, head_dim) * x_wide).astype(jnp.bfloat16)
        end_ref[:state_dim, span] = dot(b_values, weighted, ((0,), (0,))).astype(end_ref.dtype)


def project_kernel(slots, joined, order_ref, *refs):
    prompt_refs = refs[:slots]
    (local_ref, both_ref, pick_ref, inherited_ref, decay_ref, arriving_ref, tail_ref, gate_ref,
     weight_ref, down_ref, up_ref, kept_ref, sent_ref, gated, low_rank) = refs[slots:]
    models, tok_rows, inner = local_ref.shape
    head_count = decay_ref.shape[2]
    head_dim = inner // head_count
    state_dim = both_ref.shape[2] // 2
    share = tok_rows // order_ref.shape[0]
    half = models * tok_rows // 2

    @pl.when(pl.program_id(0) == 0)
    def _():
        for model in range(models):
            c_values = both_ref[model][:, state_dim:].astype(jnp.float32)
            inherited = inherited_ref[...]
            mine = dot(
                (c_values * inherited).astype(jnp.bfloat16), arriving_ref[model, :state_dim, :]
            )
            tail = jnp.broadcast_to(tail_ref[model], (8, head_count))
            sent_tail = arriving_ref[model, state_dim:, :].astype(jnp.float32)
            sent_tail = jnp.sum(sent_tail, axis=0, keepdims=True)
            borrowed = jnp.zeros((tok_rows, inner), jnp.float32)
            for slot in range(0, slots, 4):
                chosen = [c_values * pick_ref[:, i : i + 1] for i in range(slot, slot + 4)]
                states = [prompt_refs[i][model] for i in range(slot, slot + 4)]
                borrowed = borrowed + dot(
                    jnp.concatenate(chosen, axis=1).astype(jnp.bfloat16),
                    jnp.concatenate(states, axis=0),
                )
            decay = decay_ref[model]
            for first, span in head_pairs(head_count, head_dim):
                log_wide = pair_lanes(decay, first, head_dim)
                since = sent_tail[:, span] if joined else pair_lanes(tail, first, head_dim)[:1]
                log_prompt = log_wide + inherited * since
                output = (
                    local_ref[model, :, span]
                    + jnp.exp(log_wide) * mine[:, span]
                    + jnp.exp(log_prompt) * borrowed[:, span]
                )
                gate = gate_ref[model, :, span].astype(jnp.float32)
                output = (output * gate / (1.0 + jnp.exp(-gate))).astype(jnp.bfloat16)
                for quarter in range(tok_rows // share):
                    rows = pl.ds(pl.multiple_of(order_ref[quarter] + model * share, share), share)
                    gated[rows, span] = output[quarter * share : (quarter + 1) * share]
        low_rank[...] = dot(gated[...], down_ref[...]).astype(jnp.bfloat16)

    policy = lax.broadcasted_iota(jnp.int32, (models * tok_rows, 1), 0) % (models * share) < share
    adapter = jnp.where(policy, dot(low_rank[...], up_ref[...]), 0.0)
    terms = (dot(gated[...], weight_ref[...]) + adapter).astype(jnp.bfloat16)
    kept_ref[...] = terms[:half]
    sent_ref[...] = terms[half:]


def head_kernel(parts, limit_ref, *refs):
    row_refs = refs[:parts]
    weight_ref, target_ref, out_ref, held, logits_ref, arrived = refs[parts:]
    each = row_refs[0].shape[0]
    tiles, _, tile = held.shape
    copies = [
        pltpu.make_async_copy(
            weight_ref.at[:, pl.ds(i * tile, tile)], held.at[i], arrived.at[i]
        )
        for i in range(tiles)
    ]
    for copy in copies:
        copy.start()
    spans = [slice(part * each, (part + 1) * each) for part in range(parts)]
    for i in range(tiles):
        copies[i].wait()
        for rows, row_ref in zip(spans, row_refs):
            logits_ref[rows, i * tile : (i + 1) * tile] = dot(row_ref[...], held[i])
    for rows in spans:
        logits = logits_ref[rows, :]
        column = lax.broadcasted_iota(jnp.int32, logits.shape, 1)
        in_range = column < limit_ref[0]
        logits = jnp.where(in_range, logits, -jnp.inf)
        top = jnp.max(logits, axis=1, keepdims=True)
        sums = jnp.sum(jnp.exp(logits - top), axis=1, keepdims=True)
        hit = (target_ref[rows, :] - limit_ref[1] == column) & in_range
        target = jnp.sum(jnp.where(hit, logits, 0.0), axis=1, keepdims=True)
        lane = lax.broadcasted_iota(jnp.int32, (each, 128), 1)
        stats = jnp.where(lane == 0, top, jnp.where(lane == 1, sums, target))
        out_ref[:, rows] = jnp.transpose(stats)[:8]


def place_kernel(count, first_ref, *refs):
    whole, arrived = refs[count:]
    copies = []
    for i in range(count):
        blocks, size = refs[i].shape[:2]
        for j in range(blocks):
            rows = pl.ds(pl.multiple_of(first_ref[i * blocks + j], 16), size)
            copies.append(
                pltpu.make_async_copy(
                    refs[i].at[j], whole.at[rows, :], arrived.at[i * blocks + j]
                )
            )
    for copy in copies:
        copy.start()
    for copy in copies:
        copy.wait()


def norm_kernel(*refs):
    *term_refs, scale_ref, out_ref = refs
    hidden = sum(term[...].astype(jnp.float32) for term in term_refs)
    mean_sq = jnp.mean(hidden * hidden, axis=1, keepdims=True)
    out_ref[...] = (hidden * lax.rsqrt(mean_sq + 1e-05) * scale_ref[...]).astype(out_ref.dtype)


def split_kernel(head_ref, *out_refs):
    size = out_refs[0].shape[0]
    for cut, out_ref in enumerate(out_refs):
        out_ref[...] = head_ref[cut * size : (cut + 1) * size, :]


def cost(flops, moved, exps=0):
    return pl.CostEstimate(flops=flops, bytes_accessed=moved, transcendentals=exps)


def whole(value):
    return pl.BlockSpec(value.shape, lambda *_: (0,) * value.ndim)


def across(x, by):
    count = lax.axis_size("mp")
    return lax.ppermute(x, "mp", [(i, (i + 2 * by) % count ^ 1) for i in range(count)])


def shards(
    scored_token_targets,
    valid,
    lengths,
    owners,
    holders,
    mixer_input_x,
    mixer_gate_input,
    input_projection_b,
    output_projection_c,
    token_step_sizes,
    head_decay_rate,
    head_skip_scale,
    prompt_held_states,
    shared_output_weight,
    adapter_down_weight,
    adapter_up_weight,
    residual,
    final_norm_scale,
    vocab_head_weight,
):
    seq_count = lax.axis_size("seq")
    mp_count = lax.axis_size("mp")
    seq_index = lax.axis_index("seq")
    mp_index = lax.axis_index("mp")
    place = place_of(seq_index)
    core = mp_index % 2
    x_count = mp_count // 2
    x_index = mp_index // 2
    tok_rows = scored_token_targets.shape[0]
    models = mixer_input_x.shape[0]
    inner_local = mixer_input_x.shape[2]
    head_count = token_step_sizes.shape[2]
    state_dim = input_projection_b.shape[2]
    roll_count = lengths.shape[0]
    width = residual.shape[2]
    blocks = seq_count // (CHAIN * SIDE)
    partners = list(itertools.product(range(SIDE), range(blocks)))[1:]
    share_rows = tok_rows // mp_count

    def from_partner(side, block):
        return partner(seq_index, side, blocks - block, seq_count)

    def beside(value):
        return [to_partner(value, side, block) for side, block in partners]

    held = jnp.transpose(prompt_held_states[:, 0], (0, 3, 1, 2)).reshape(
        models, state_dim, inner_local
    )
    states = [held, turn(held, 1), turn(held, 2)]
    states.append(turn(states[2], 1))
    beside_held = beside(held)

    first_row = seq_index * tok_rows
    offsets = jnp.arange(tok_rows, dtype=jnp.int32)
    position = first_row + offsets
    starts = jnp.cumsum(lengths) - lengths
    rollout = jnp.sum((starts[None, :] <= position[:, None]).astype(jnp.int32), axis=1) - 1
    member_table = rollout[:, None] == jnp.arange(roll_count, dtype=jnp.int32)[None, :]
    start_local = jnp.sum(jnp.where(member_table, starts[None, :], 0), axis=1) - first_row
    holder_tok = jnp.sum(jnp.where(member_table, holders[None, :], 0), axis=1)
    prompt_holder = jnp.stack(
        [
            turned(source, k)
            for k in range(CHAIN)
            for source in [seq_index] + [from_partner(side, block) for side, block in partners]
        ]
    )
    both_projections = jnp.concatenate([input_projection_b, output_projection_c], axis=2)
    pick = (holder_tok[:, None] == prompt_holder[None, :]).astype(jnp.float32)
    inherited = (start_local < 0).astype(jnp.float32)
    beside_next = beside(states[1])
    mixer_x, states[1], *beside_held = tied(mixer_input_x, states[1], *beside_held)

    per_model = lambda *shape: pl.BlockSpec((None,) + shape, lambda m: (m,) + (0,) * len(shape))
    local_out, local_end, decay = pl.pallas_call(
        local_kernel,
        grid=(models,),
        in_specs=[
            per_model(tok_rows, inner_local),
            per_model(tok_rows, 2 * state_dim),
            per_model(tok_rows, head_count),
            per_model(1, head_count),
            pl.BlockSpec((tok_rows, 1), lambda m: (0, 0)),
            per_model(1, head_count),
        ],
        out_specs=[
            per_model(tok_rows, inner_local),
            per_model(state_dim + TAIL_ROWS, inner_local),
            per_model(tok_rows, head_count),
        ],
        out_shape=[
            jax.ShapeDtypeStruct((models, tok_rows, inner_local), jnp.float32),
            jax.ShapeDtypeStruct((models, state_dim + TAIL_ROWS, inner_local), jnp.bfloat16),
            jax.ShapeDtypeStruct((models, tok_rows, head_count), jnp.float32),
        ],
        compiler_params=pltpu.CompilerParams(vmem_limit_bytes=32 * 2**20),
        cost_estimate=cost(10**9, 8 * 2**20, 2 * 10**6),
        name="local_tokens",
    )(
        mixer_x,
        both_projections,
        token_step_sizes,
        head_decay_rate[:, None, :],
        start_local[:, None],
        head_skip_scale[:, None, :],
    )

    hops = max(1, -(-(seq_count * tok_rows // 8) // tok_rows))
    next_one = [(i, i + 1) for i in range(seq_count - 1)]
    arriving = lax.ppermute(local_end, "seq", next_one)
    tail = jnp.zeros((models, head_count), jnp.float32)
    if hops > 1:
        local_tail = decay[:, -1]
        tail = lax.ppermute(local_tail, "seq", next_one)
        through = jnp.repeat(jnp.exp(local_tail), inner_local // head_count, axis=1)
        through = through[:, None, :] * inherited[-1]
        for _ in range(hops - 1):
            moved = through * arriving.astype(jnp.float32) + local_end.astype(jnp.float32)
            arriving = lax.ppermute(moved.astype(jnp.bfloat16), "seq", next_one)
            tail = lax.ppermute(inherited[-1] * tail + local_tail, "seq", next_one)

    head_rows, vocab_local = vocab_head_weight.shape
    part = -(-vocab_local // (CHAIN * 128)) * 128
    cuts = 2 if head_rows % 32 == 0 else 1
    cut_rows = head_rows // cuts
    head = pl.pallas_call(
        split_kernel,
        grid=(CHAIN,),
        in_specs=[pl.BlockSpec((head_rows, part), lambda j: (0, j))],
        out_specs=[pl.BlockSpec((None, cut_rows, part), lambda j: (j, 0, 0))] * cuts,
        out_shape=[jax.ShapeDtypeStruct((CHAIN, cut_rows, part), vocab_head_weight.dtype)] * cuts,
        cost_estimate=cost(0, 2 * vocab_head_weight.size * 2),
        name="split_head_columns",
    )(vocab_head_weight)
    arriving, states[3], *head = tied(arriving, states[3], *head)
    came_head = [
        lax.all_to_all(head[cut], "seq", 0, 0, axis_index_groups=chain_groups())
        for cut in range(cuts)
    ]

    besides = [beside_held, beside_next, beside(states[2]), beside(states[3])]
    prompts = []
    for state, others in zip(states, besides):
        prompts += [state] + list(others)

    quarter = jnp.arange(mp_count, dtype=jnp.int32)
    order = (quarter % 2 != core) * x_count + (quarter // 2 - x_index) % x_count
    order = order.astype(jnp.int32) * (models * share_rows)
    half = models * tok_rows // 2
    tile = 512 if width % 512 == 0 else width
    resident = [
        *prompts,
        local_out,
        both_projections,
        pick,
        inherited[:, None],
        decay,
        arriving,
        tail[:, None, :],
        mixer_gate_input,
    ]
    kept, sent = pl.pallas_call(
        functools.partial(project_kernel, len(prompts), hops == 1),
        grid=(width // tile,),
        in_specs=[pl.BlockSpec(memory_space=pltpu.SMEM)]
        + [whole(value) for value in resident]
        + [
            pl.BlockSpec((inner_local, tile), lambda j: (0, j)),
            whole(adapter_down_weight),
            pl.BlockSpec((adapter_up_weight.shape[0], tile), lambda j: (0, j)),
        ],
        out_specs=[pl.BlockSpec((half, tile), lambda j: (0, j))] * 2,
        out_shape=[jax.ShapeDtypeStruct((half, width), jnp.bfloat16)] * 2,
        scratch_shapes=[
            pltpu.VMEM((models * tok_rows, inner_local), jnp.bfloat16),
            pltpu.VMEM((models * tok_rows, adapter_up_weight.shape[0]), jnp.bfloat16),
        ],
        compiler_params=pltpu.CompilerParams(vmem_limit_bytes=56 * 2**20),
        cost_estimate=cost(
            2 * models * tok_rows * inner_local * width, 4 * inner_local * width, 2 * 10**6
        ),
        name="gate_and_project",
    )(order, *resident, shared_output_weight, adapter_down_weight, adapter_up_weight)

    own_words = jnp.stack([scored_token_targets, valid])
    sent, came_head[0], own_words = tied(sent, came_head[0], own_words)
    words_and_valid = [own_words] + [turn(own_words, k) for k in range(1, CHAIN)]
    came = other_core(sent)
    each = models * share_rows

    def chip_sum(by):
        rows = slice(by * each, (by + 1) * each)
        return kept[rows].astype(jnp.float32) + came[rows].astype(jnp.float32)

    own_rows = lax.dynamic_slice_in_dim(residual, mp_index * share_rows, share_rows, 0)
    own_rows = jnp.transpose(own_rows, (1, 0, 2)).reshape(each, width)
    crossing = [along_x(chip_sum(by).astype(jnp.bfloat16), by) for by in range(1, x_count)]
    besides_head = [beside(came_head[0])]
    half_block = pl.BlockSpec((each, width), lambda i: (0, 0))
    normed_own = pl.pallas_call(
        norm_kernel,
        grid=(1,),
        in_specs=[half_block] * (3 + len(crossing)) + [pl.BlockSpec((1, width), lambda i: (0, 0))],
        out_specs=half_block,
        out_shape=jax.ShapeDtypeStruct((each, width), jnp.bfloat16),
        compiler_params=pltpu.CompilerParams(vmem_limit_bytes=32 * 2**20),
        cost_estimate=cost(0, width),
        name="add_and_norm",
    )(own_rows, kept, came, *crossing, final_norm_scale[None, :])
    normed_own, came_head[-1], *words_and_valid = tied(
        normed_own, came_head[-1], *words_and_valid
    )
    words_and_valid = jnp.stack(words_and_valid)
    besides_head += [beside(piece) for piece in came_head[1:]]

    limit = jnp.stack(
        [
            jnp.minimum(vocab_local - place * part, part),
            mp_index * vocab_local + place * part,
        ]
    ).astype(jnp.int32)
    mp_order = jnp.stack(
        [(x_index - k) % x_count * 2 + (core + other) % 2 for other in (0, 1) for k in range(x_count)]
    )

    def words_of(targets):
        targets = targets.reshape(CHAIN, mp_count, 1, share_rows)[:, mp_order]
        targets = jnp.broadcast_to(targets, (CHAIN, mp_count, models, share_rows))
        return targets.reshape(CHAIN, 2, x_count, each)

    tiles = 2 if part % 256 == 0 else 1

    def place_head():
        pieces, firsts = [], []
        for cut, others in enumerate(besides_head):
            pieces += [came_head[cut]] + others
            for source in [seq_index] + [from_partner(side, block) for side, block in partners]:
                first_of_chain = source - place_of(source) * SIDE
                firsts += [
                    (first_of_chain + k * SIDE) * head_rows + cut * cut_rows for k in range(CHAIN)
                ]
        return pl.pallas_call(
            functools.partial(place_kernel, len(pieces)),
            in_specs=[pl.BlockSpec(memory_space=pltpu.SMEM)]
            + [pl.BlockSpec(memory_space=pl.ANY)] * len(pieces),
            out_specs=pl.BlockSpec(memory_space=pltpu.VMEM),
            out_shape=jax.ShapeDtypeStruct((seq_count * head_rows, part), vocab_head_weight.dtype),
            scratch_shapes=[pltpu.SemaphoreType.DMA((len(pieces) * CHAIN,))],
            compiler_params=pltpu.CompilerParams(vmem_limit_bytes=16 * 2**20),
            cost_estimate=cost(0, 4 * seq_count * head_rows * part),
            name="place_head_rows",
        )(jnp.stack(firsts).astype(jnp.int32), *pieces)

    def head_stats(head_part, rows, words):
        count = len(rows)
        words = words.reshape(count * each, 1)
        stats_shape = jax.ShapeDtypeStruct((8, count * each), jnp.float32)
        return pl.pallas_call(
            functools.partial(head_kernel, count),
            in_specs=[pl.BlockSpec(memory_space=pltpu.SMEM)]
            + [pl.BlockSpec(memory_space=pltpu.VMEM)] * count
            + [pl.BlockSpec(memory_space=pl.ANY), pl.BlockSpec(memory_space=pltpu.VMEM)],
            out_specs=pl.BlockSpec(memory_space=pltpu.VMEM),
            out_shape=stats_shape,
            scratch_shapes=[
                pltpu.VMEM((tiles, width, part // tiles), jnp.bfloat16),
                pltpu.VMEM((count * each, part), jnp.float32),
                pltpu.SemaphoreType.DMA((tiles,)),
            ],
            compiler_params=pltpu.CompilerParams(vmem_limit_bytes=56 * 2**20),
            cost_estimate=cost(
                2 * count * each * width * part,
                2 * (count * each + part) * width,
                count * each * part,
            ),
            name="head_stats",
        )(limit, *rows, head_part, words).reshape(8, count, models, share_rows)

    def both_cores(values):
        return values + [other_core(value) for value in values]

    def crossed(rows):
        return [along_x(rows, by) for by in range(1, x_count)]

    blocks_of = [normed_own]
    nears = [crossed(normed_own)]
    words = words_of(words_and_valid[:, 0])
    at_end = (place == 0) | (place == CHAIN - 1)
    for step in range(1, CHAIN):
        if step == 1:
            moved = [turn(normed_own, 1), between(normed_own, [(1, 2), (2, 1)])]
        elif step == 2:
            moved = [between(inner, [(1, 0), (2, 3)]), between(blocks_of[1], [(1, 2), (2, 1)])]
        else:
            moved = [between(passed, [(1, 0), (2, 3)])]
        count = len(nears[-1])
        extra = []
        if step == 1:
            extra = besides_head[0]
        elif step == CHAIN - 2:
            extra = besides_head[-1]
        elif step == CHAIN - 1:
            head_part = place_head()
            rows = both_cores([blocks_of[0]] + nears[0])
            extra = [head_stats(head_part, rows, words[0])]
        came = tied(*nears[-1], *extra, *moved)
        nears[-1], extra, moved = came[:count], came[count : -len(moved)], came[-len(moved) :]
        if step == 1:
            besides_head[0] = extra
        elif step == CHAIN - 2:
            besides_head[-1] = extra
        elif step == CHAIN - 1:
            early = extra[0]
        if step == 1:
            block, inner = moved
        elif step == 2:
            passed = moved[1]
            block = jnp.where(at_end, moved[0], passed)
        else:
            block = jnp.where(at_end, moved[0], inner)
        blocks_of.append(block)
        nears.append(crossed(block))

    last = CHAIN - 1
    rows = [both_cores([blocks_of[k]] + nears[k]) for k in range(1, last)]
    middle = head_stats(
        head_part,
        [value for values in rows for value in values] + both_cores([blocks_of[last]]),
        jnp.concatenate([words[1:last].reshape(-1, each), words[last, :, 0]]),
    )
    def blocks(stats):
        return stats[:3].reshape(3, -1, 2, x_count, models, share_rows)

    *nears[last], middle, early = tied(*nears[last], middle, early)
    rest = head_stats(head_part, both_cores(nears[last]), words[last, :, 1:])
    whole_blocks = (last - 1) * mp_count
    own_side = middle[:3, whole_blocks:].reshape(3, 1, 2, 1, models, share_rows)
    other_side = rest[:3].reshape(3, 1, 2, x_count - 1, models, share_rows)
    stats = jnp.concatenate(
        [
            blocks(early),
            blocks(middle[:, :whole_blocks]),
            jnp.concatenate([own_side, other_side], axis=3),
        ],
        axis=1,
    )

    def merged(several):
        top = functools.reduce(jnp.maximum, [stats[0] for stats in several])
        total = sum(stats[1] * jnp.exp(stats[0] - top) for stats in several)
        return jnp.stack([top, total, sum(stats[2] for stats in several)])

    several = [stats]
    for by in range(1, CHAIN):
        came = turn(stats, by)
        several.append(jnp.stack([came[:, k ^ by] for k in range(CHAIN)], axis=1))
    stats = merged(several)
    several = [stats, other_core(stats)[:, :, ::-1]]
    for by in range(1, x_count):
        several.append(jnp.roll(along_x(stats, by), by, axis=3))
        several.append(jnp.roll(across(stats, by)[:, :, ::-1], by, axis=3))
    stats = merged(several)
    logprob = stats[2] - stats[0] - jnp.log(stats[1])
    delta = (logprob[:, :, :, 0] - logprob[:, :, :, 1]).reshape(CHAIN, mp_count, share_rows)
    in_order = mp_order[None, :] == quarter[:, None]
    delta = jnp.sum(jnp.where(in_order[None, :, :, None], delta[:, None], 0.0), axis=2)
    delta = delta.reshape(CHAIN, tok_rows) * words_and_valid[:, 1].astype(jnp.float32)
    token_delta = delta[0]
    first_rows = jnp.stack([turned(seq_index, k) for k in range(CHAIN)]) * tok_rows
    since = (first_rows[:, None] + offsets[None, :])[:, :, None] - starts
    member = ((since >= 0) & (since < lengths)).astype(jnp.float32)
    roll_sums = jnp.dot(
        delta.reshape(-1), member.reshape(-1, roll_count), precision=highest
    )
    roll_sums = roll_sums + sum(beside(roll_sums))
    owner_sums = jnp.where(owners == seq_index, roll_sums / lengths.astype(jnp.float32), 0.0)
    return (owner_sums[None, :], token_delta)


def solution(mesh):
    placed = (
        P("seq"),
        P("seq"),
        P(),
        P(),
        P(),
        P(None, "seq", "mp"),
        P(None, "seq", "mp"),
        P(None, "seq", None),
        P(None, "seq", None),
        P(None, "seq", "mp"),
        P(None, "mp"),
        P(None, "mp"),
        P(None, "seq", "mp", None, None),
        P("mp", None),
        P("mp", None),
        P(),
        P("seq", None, None),
        P(),
        P("seq", "mp"),
    )
    return jax.shard_map(
        shards, mesh=mesh, in_specs=placed, out_specs=(P("seq", None), P("seq")), check_vma=False
    )
```

```python
import functools
import itertools

import jax
import jax.numpy as jnp
from jax import lax
from jax.experimental import pallas as pl
from jax.experimental.pallas import tpu as pltpu
from jax.sharding import PartitionSpec as P

highest = lax.Precision.HIGHEST
CHAIN = 4
TAIL_ROWS = 16
SIDE = 2


def place_of(i):
    return (i // SIDE) % CHAIN


def turned(i, by):
    return i ^ (by * SIDE)


def partner(i, side, block, count):
    return ((i ^ side) + block * CHAIN * SIDE) % count


def turn(x, by):
    count = lax.axis_size("seq")
    return lax.ppermute(x, "seq", [(i, turned(i, by)) for i in range(count)])


def to_partner(x, side, block):
    count = lax.axis_size("seq")
    return lax.ppermute(x, "seq", [(i, partner(i, side, block, count)) for i in range(count)])


def between(x, pairs):
    count = lax.axis_size("seq")
    sends = [
        (i, i + (to - place) * SIDE)
        for i in range(count)
        for place, to in pairs
        if place_of(i) == place
    ]
    return lax.ppermute(x, "seq", sends)


def chain_groups():
    count = lax.axis_size("seq")
    return [
        [first + k * SIDE for k in range(CHAIN)] for first in range(count) if place_of(first) == 0
    ]


def other_core(x):
    count = lax.axis_size("mp")
    return lax.ppermute(x, "mp", [(i, i ^ 1) for i in range(count)])


def along_x(x, by):
    count = lax.axis_size("mp")
    return lax.ppermute(x, "mp", [(i, (i + 2 * by) % count) for i in range(count)])


def tied(*values):
    return list(lax.optimization_barrier(values))


def dot(a, b, over=((1,), (0,))):
    return lax.dot_general(a, b, (over, ((), ())), preferred_element_type=jnp.float32)


def exact(a, b):
    return lax.dot_general(
        a, b, (((1,), (0,)), ((), ())), precision=highest, preferred_element_type=jnp.float32
    )


def head_pairs(head_count, head_dim):
    return [
        (first, slice(first * head_dim, min(first + 2, head_count) * head_dim))
        for first in range(0, head_count, 2)
    ]


def pair_lanes(values, first, head_dim):
    if first + 1 == values.shape[1]:
        return jnp.broadcast_to(values[:, first : first + 1], (values.shape[0], head_dim))
    lane = lax.broadcasted_iota(jnp.int32, (values.shape[0], 2 * head_dim), 1)
    return jnp.where(lane < head_dim, values[:, first : first + 1], values[:, first + 1 : first + 2])


def local_kernel(
    x_ref, both_ref, step_ref, rate_ref, start_ref, skip_ref, out_ref, end_ref, decay_ref,
):
    tok_rows, inner = x_ref.shape
    head_count = step_ref.shape[1]
    head_dim = inner // head_count
    state_dim = both_ref.shape[1] // 2
    b_values, c_values = both_ref[:, :state_dim], both_ref[:, state_dim:]
    row = lax.broadcasted_iota(jnp.int32, (tok_rows, tok_rows), 0)
    col = lax.broadcasted_iota(jnp.int32, (tok_rows, tok_rows), 1)
    causal = (col >= start_ref[...]) & (col <= row)
    gram = jnp.where(causal, dot(c_values, b_values, ((1,), (1,))), 0.0)
    steps = step_ref[...]
    logs = exact(jnp.where(col <= row, 1.0, 0.0), -steps * rate_ref[...])
    decay = logs - exact(jnp.where(col == start_ref[...] - 1, 1.0, 0.0), logs)
    decay_ref[...] = decay
    since = jnp.broadcast_to(decay[tok_rows - 1 :, :], (TAIL_ROWS, head_count))
    term = lax.broadcasted_iota(jnp.int32, since.shape, 0)
    high = since.astype(jnp.bfloat16).astype(jnp.float32)
    middle = (since - high).astype(jnp.bfloat16).astype(jnp.float32)
    low = since - high - middle
    since = jnp.where(term == 0, high, jnp.where(term == 1, middle, jnp.where(term == 2, low, 0.0)))
    fill = jnp.zeros((tok_rows, 128 - 2 * head_count), jnp.float32)
    as_rows = jnp.transpose(jnp.concatenate([logs, steps, fill], axis=1))
    last_log = logs[tok_rows - 1 :, :]
    last_start = start_ref[tok_rows - 1 :, :]
    place = lax.broadcasted_iota(jnp.int32, (tok_rows, 1), 0)
    weight = jnp.where(place >= last_start, jnp.exp(last_log - logs) * steps, 0.0)
    skip = jnp.broadcast_to(skip_ref[...], (8, head_count))
    for first, span in head_pairs(head_count, head_dim):
        x_pair = x_ref[:, span]
        sides = []
        for head in range(first, min(first + 2, head_count)):
            gap = jnp.minimum(logs[:, head : head + 1] - as_rows[head : head + 1, :], 0.0)
            mixing = jnp.exp(gap) * gram * as_rows[head_count + head : head_count + head + 1, :]
            sides.append(dot(mixing.astype(jnp.bfloat16), x_pair))
        x_wide = x_pair.astype(jnp.float32)
        lane = lax.broadcasted_iota(jnp.int32, x_pair.shape, 1)
        out_ref[:, span] = (
            jnp.where(lane < head_dim, sides[0], sides[-1])
            + pair_lanes(skip, first, head_dim)[:1] * x_wide
        )
        tail = pair_lanes(since, first, head_dim)
        end_ref[state_dim:, span] = tail.astype(end_ref.dtype)
        weighted = (pair_lanes(weight, first, head_dim) * x_wide).astype(jnp.bfloat16)
        end_ref[:state_dim, span] = dot(b_values, weighted, ((0,), (0,))).astype(end_ref.dtype)


def project_kernel(slots, joined, order_ref, *refs):
    prompt_refs = refs[:slots]
    (local_ref, both_ref, pick_ref, inherited_ref, decay_ref, arriving_ref, tail_ref, gate_ref,
     weight_ref, down_ref, up_ref, kept_ref, sent_ref, gated, low_rank) = refs[slots:]
    models, tok_rows, inner = local_ref.shape
    head_count = decay_ref.shape[2]
    head_dim = inner // head_count
    state_dim = both_ref.shape[2] // 2
    share = tok_rows // order_ref.shape[0]
    half = models * tok_rows // 2

    @pl.when(pl.program_id(0) == 0)
    def _():
        for model in range(models):
            c_values = both_ref[model][:, state_dim:].astype(jnp.float32)
            inherited = inherited_ref[...]
            mine = dot(
                (c_values * inherited).astype(jnp.bfloat16), arriving_ref[model, :state_dim, :]
            )
            tail = jnp.broadcast_to(tail_ref[model], (8, head_count))
            sent_tail = arriving_ref[model, state_dim:, :].astype(jnp.float32)
            sent_tail = jnp.sum(sent_tail, axis=0, keepdims=True)
            borrowed = jnp.zeros((tok_rows, inner), jnp.float32)
            for slot in range(0, slots, 4):
                chosen = [c_values * pick_ref[:, i : i + 1] for i in range(slot, slot + 4)]
                states = [prompt_refs[i][model] for i in range(slot, slot + 4)]
                borrowed = borrowed + dot(
                    jnp.concatenate(chosen, axis=1).astype(jnp.bfloat16),
                    jnp.concatenate(states, axis=0),
                )
            decay = decay_ref[model]
            for first, span in head_pairs(head_count, head_dim):
                log_wide = pair_lanes(decay, first, head_dim)
                since = sent_tail[:, span] if joined else pair_lanes(tail, first, head_dim)[:1]
                log_prompt = log_wide + inherited * since
                output = (
                    local_ref[model, :, span]
                    + jnp.exp(log_wide) * mine[:, span]
                    + jnp.exp(log_prompt) * borrowed[:, span]
                )
                gate = gate_ref[model, :, span].astype(jnp.float32)
                output = (output * gate / (1.0 + jnp.exp(-gate))).astype(jnp.bfloat16)
                for quarter in range(tok_rows // share):
                    rows = pl.ds(pl.multiple_of(order_ref[quarter] + model * share, share), share)
                    gated[rows, span] = output[quarter * share : (quarter + 1) * share]
        low_rank[...] = dot(gated[...], down_ref[...]).astype(jnp.bfloat16)

    policy = lax.broadcasted_iota(jnp.int32, (models * tok_rows, 1), 0) % (models * share) < share
    adapter = jnp.where(policy, dot(low_rank[...], up_ref[...]), 0.0)
    terms = (dot(gated[...], weight_ref[...]) + adapter).astype(jnp.bfloat16)
    kept_ref[...] = terms[:half]
    sent_ref[...] = terms[half:]


def head_kernel(parts, limit_ref, *refs):
    row_refs = refs[:parts]
    weight_ref, target_ref, out_ref, held, logits_ref, arrived = refs[parts:]
    each = row_refs[0].shape[0]
    tiles, _, tile = held.shape
    copies = [
        pltpu.make_async_copy(
            weight_ref.at[:, pl.ds(i * tile, tile)], held.at[i], arrived.at[i]
        )
        for i in range(tiles)
    ]
    for copy in copies:
        copy.start()
    spans = [slice(part * each, (part + 1) * each) for part in range(parts)]
    for i in range(tiles):
        copies[i].wait()
        for rows, row_ref in zip(spans, row_refs):
            logits_ref[rows, i * tile : (i + 1) * tile] = dot(row_ref[...], held[i])
    for rows in spans:
        logits = logits_ref[rows, :]
        column = lax.broadcasted_iota(jnp.int32, logits.shape, 1)
        in_range = column < limit_ref[0]
        logits = jnp.where(in_range, logits, -jnp.inf)
        top = jnp.max(logits, axis=1, keepdims=True)
        sums = jnp.sum(jnp.exp(logits - top), axis=1, keepdims=True)
        hit = (target_ref[rows, :] - limit_ref[1] == column) & in_range
        target = jnp.sum(jnp.where(hit, logits, 0.0), axis=1, keepdims=True)
        lane = lax.broadcasted_iota(jnp.int32, (each, 128), 1)
        stats = jnp.where(lane == 0, top, jnp.where(lane == 1, sums, target))
        out_ref[:, rows] = jnp.transpose(stats)[:8]


def place_kernel(count, first_ref, *refs):
    whole, arrived = refs[count:]
    copies = []
    for i in range(count):
        blocks, size = refs[i].shape[:2]
        for j in range(blocks):
            rows = pl.ds(pl.multiple_of(first_ref[i * blocks + j], 16), size)
            copies.append(
                pltpu.make_async_copy(
                    refs[i].at[j], whole.at[rows, :], arrived.at[i * blocks + j]
                )
            )
    for copy in copies:
        copy.start()
    for copy in copies:
        copy.wait()


def norm_kernel(*refs):
    *term_refs, scale_ref, out_ref = refs
    hidden = sum(term[...].astype(jnp.float32) for term in term_refs)
    mean_sq = jnp.mean(hidden * hidden, axis=1, keepdims=True)
    out_ref[...] = (hidden * lax.rsqrt(mean_sq + 1e-05) * scale_ref[...]).astype(out_ref.dtype)


def split_kernel(head_ref, *out_refs):
    columns = head_ref.shape[1]
    blocks, size, part = out_refs[0].shape
    for cut, out_ref in enumerate(out_refs):
        rows = slice(cut * size, (cut + 1) * size)
        for block in range(blocks):
            first = block * part
            count = min(part, columns - first)
            out_ref[block, :, :count] = head_ref[rows, first : first + count]
            if count < part:
                out_ref[block, :, count:] = jnp.zeros((size, part - count), out_ref.dtype)


def cost(flops, moved, exps=0):
    return pl.CostEstimate(flops=flops, bytes_accessed=moved, transcendentals=exps)


def whole(value):
    return pl.BlockSpec(value.shape, lambda *_: (0,) * value.ndim)


def across(x, by):
    count = lax.axis_size("mp")
    return lax.ppermute(x, "mp", [(i, (i + 2 * by) % count ^ 1) for i in range(count)])


def shards(
    scored_token_targets,
    valid,
    lengths,
    owners,
    holders,
    mixer_input_x,
    mixer_gate_input,
    input_projection_b,
    output_projection_c,
    token_step_sizes,
    head_decay_rate,
    head_skip_scale,
    prompt_held_states,
    shared_output_weight,
    adapter_down_weight,
    adapter_up_weight,
    residual,
    final_norm_scale,
    vocab_head_weight,
):
    seq_count = lax.axis_size("seq")
    mp_count = lax.axis_size("mp")
    seq_index = lax.axis_index("seq")
    mp_index = lax.axis_index("mp")
    place = place_of(seq_index)
    core = mp_index % 2
    x_count = mp_count // 2
    x_index = mp_index // 2
    tok_rows = scored_token_targets.shape[0]
    models = mixer_input_x.shape[0]
    inner_local = mixer_input_x.shape[2]
    head_count = token_step_sizes.shape[2]
    state_dim = input_projection_b.shape[2]
    roll_count = lengths.shape[0]
    width = residual.shape[2]
    blocks = seq_count // (CHAIN * SIDE)
    partners = list(itertools.product(range(SIDE), range(blocks)))[1:]
    share_rows = tok_rows // mp_count

    def from_partner(side, block):
        return partner(seq_index, side, blocks - block, seq_count)

    def beside(value):
        return [to_partner(value, side, block) for side, block in partners]

    held = jnp.transpose(prompt_held_states[:, 0], (0, 3, 1, 2)).reshape(
        models, state_dim, inner_local
    )
    states = [held, turn(held, 1), turn(held, 2)]
    states.append(turn(states[2], 1))
    beside_held = beside(held)

    first_row = seq_index * tok_rows
    offsets = jnp.arange(tok_rows, dtype=jnp.int32)
    position = first_row + offsets
    starts = jnp.cumsum(lengths) - lengths
    rollout = jnp.sum((starts[None, :] <= position[:, None]).astype(jnp.int32), axis=1) - 1
    member_table = rollout[:, None] == jnp.arange(roll_count, dtype=jnp.int32)[None, :]
    start_local = jnp.sum(jnp.where(member_table, starts[None, :], 0), axis=1) - first_row
    holder_tok = jnp.sum(jnp.where(member_table, holders[None, :], 0), axis=1)
    prompt_holder = jnp.stack(
        [
            turned(source, k)
            for k in range(CHAIN)
            for source in [seq_index] + [from_partner(side, block) for side, block in partners]
        ]
    )
    both_projections = jnp.concatenate([input_projection_b, output_projection_c], axis=2)
    pick = (holder_tok[:, None] == prompt_holder[None, :]).astype(jnp.float32)
    inherited = (start_local < 0).astype(jnp.float32)
    beside_next = beside(states[1])
    mixer_x, states[1], *beside_held = tied(mixer_input_x, states[1], *beside_held)

    per_model = lambda *shape: pl.BlockSpec((None,) + shape, lambda m: (m,) + (0,) * len(shape))
    local_out, local_end, decay = pl.pallas_call(
        local_kernel,
        grid=(models,),
        in_specs=[
            per_model(tok_rows, inner_local),
            per_model(tok_rows, 2 * state_dim),
            per_model(tok_rows, head_count),
            per_model(1, head_count),
            pl.BlockSpec((tok_rows, 1), lambda m: (0, 0)),
            per_model(1, head_count),
        ],
        out_specs=[
            per_model(tok_rows, inner_local),
            per_model(state_dim + TAIL_ROWS, inner_local),
            per_model(tok_rows, head_count),
        ],
        out_shape=[
            jax.ShapeDtypeStruct((models, tok_rows, inner_local), jnp.float32),
            jax.ShapeDtypeStruct((models, state_dim + TAIL_ROWS, inner_local), jnp.bfloat16),
            jax.ShapeDtypeStruct((models, tok_rows, head_count), jnp.float32),
        ],
        compiler_params=pltpu.CompilerParams(vmem_limit_bytes=32 * 2**20),
        cost_estimate=cost(10**9, 8 * 2**20, 2 * 10**6),
        name="local_tokens",
    )(
        mixer_x,
        both_projections,
        token_step_sizes,
        head_decay_rate[:, None, :],
        start_local[:, None],
        head_skip_scale[:, None, :],
    )

    hops = max(1, -(-(seq_count * tok_rows // 8) // tok_rows))
    next_one = [(i, i + 1) for i in range(seq_count - 1)]
    arriving = lax.ppermute(local_end, "seq", next_one)
    tail = jnp.zeros((models, head_count), jnp.float32)
    if hops > 1:
        local_tail = decay[:, -1]
        tail = lax.ppermute(local_tail, "seq", next_one)
        through = jnp.repeat(jnp.exp(local_tail), inner_local // head_count, axis=1)
        through = through[:, None, :] * inherited[-1]
        for _ in range(hops - 1):
            moved = through * arriving.astype(jnp.float32) + local_end.astype(jnp.float32)
            arriving = lax.ppermute(moved.astype(jnp.bfloat16), "seq", next_one)
            tail = lax.ppermute(inherited[-1] * tail + local_tail, "seq", next_one)

    head_rows, vocab_local = vocab_head_weight.shape
    part = -(-vocab_local // (CHAIN * 128)) * 128
    cuts = 2 if head_rows % 32 == 0 else 1
    cut_rows = head_rows // cuts
    head = pl.pallas_call(
        split_kernel,
        grid=(1,),
        in_specs=[whole(vocab_head_weight)],
        out_specs=[pl.BlockSpec((CHAIN, cut_rows, part), lambda j: (0, 0, 0))] * cuts,
        out_shape=[jax.ShapeDtypeStruct((CHAIN, cut_rows, part), vocab_head_weight.dtype)] * cuts,
        compiler_params=pltpu.CompilerParams(vmem_limit_bytes=32 * 2**20),
        cost_estimate=cost(0, 2 * vocab_head_weight.size * 2),
        name="split_head_columns",
    )(vocab_head_weight)
    arriving, states[3], *head = tied(arriving, states[3], *head)
    came_head = [
        lax.all_to_all(head[cut], "seq", 0, 0, axis_index_groups=chain_groups())
        for cut in range(cuts)
    ]

    besides = [beside_held, beside_next, beside(states[2]), beside(states[3])]
    prompts = []
    for state, others in zip(states, besides):
        prompts += [state] + list(others)

    quarter = jnp.arange(mp_count, dtype=jnp.int32)
    order = (quarter % 2 != core) * x_count + (quarter // 2 - x_index) % x_count
    order = order.astype(jnp.int32) * (models * share_rows)
    half = models * tok_rows // 2
    tile = 512 if width % 512 == 0 else width
    resident = [
        *prompts,
        local_out,
        both_projections,
        pick,
        inherited[:, None],
        decay,
        arriving,
        tail[:, None, :],
        mixer_gate_input,
    ]
    kept, sent = pl.pallas_call(
        functools.partial(project_kernel, len(prompts), hops == 1),
        grid=(width // tile,),
        in_specs=[pl.BlockSpec(memory_space=pltpu.SMEM)]
        + [whole(value) for value in resident]
        + [
            pl.BlockSpec((inner_local, tile), lambda j: (0, j)),
            whole(adapter_down_weight),
            pl.BlockSpec((adapter_up_weight.shape[0], tile), lambda j: (0, j)),
        ],
        out_specs=[pl.BlockSpec((half, tile), lambda j: (0, j))] * 2,
        out_shape=[jax.ShapeDtypeStruct((half, width), jnp.bfloat16)] * 2,
        scratch_shapes=[
            pltpu.VMEM((models * tok_rows, inner_local), jnp.bfloat16),
            pltpu.VMEM((models * tok_rows, adapter_up_weight.shape[0]), jnp.bfloat16),
        ],
        compiler_params=pltpu.CompilerParams(vmem_limit_bytes=56 * 2**20),
        cost_estimate=cost(
            2 * models * tok_rows * inner_local * width, 4 * inner_local * width, 2 * 10**6
        ),
        name="gate_and_project",
    )(order, *resident, shared_output_weight, adapter_down_weight, adapter_up_weight)

    own_words = jnp.stack([scored_token_targets, valid])
    sent, came_head[0], own_words = tied(sent, came_head[0], own_words)
    words_and_valid = [own_words] + [turn(own_words, k) for k in range(1, CHAIN)]
    came = other_core(sent)
    each = models * share_rows

    def chip_sum(by):
        rows = slice(by * each, (by + 1) * each)
        return kept[rows].astype(jnp.float32) + came[rows].astype(jnp.float32)

    own_rows = lax.dynamic_slice_in_dim(residual, mp_index * share_rows, share_rows, 0)
    own_rows = jnp.transpose(own_rows, (1, 0, 2)).reshape(each, width)
    crossing = [along_x(chip_sum(by).astype(jnp.bfloat16), by) for by in range(1, x_count)]
    besides_head = [beside(came_head[0])]
    half_block = pl.BlockSpec((each, width), lambda i: (0, 0))
    normed_own = pl.pallas_call(
        norm_kernel,
        grid=(1,),
        in_specs=[half_block] * (3 + len(crossing)) + [pl.BlockSpec((1, width), lambda i: (0, 0))],
        out_specs=half_block,
        out_shape=jax.ShapeDtypeStruct((each, width), jnp.bfloat16),
        compiler_params=pltpu.CompilerParams(vmem_limit_bytes=32 * 2**20),
        cost_estimate=cost(0, width),
        name="add_and_norm",
    )(own_rows, kept, came, *crossing, final_norm_scale[None, :])
    normed_own, came_head[-1], *words_and_valid = tied(
        normed_own, came_head[-1], *words_and_valid
    )
    words_and_valid = jnp.stack(words_and_valid)
    besides_head += [beside(piece) for piece in came_head[1:]]

    limit = jnp.stack(
        [
            jnp.minimum(vocab_local - place * part, part),
            mp_index * vocab_local + place * part,
        ]
    ).astype(jnp.int32)
    mp_order = jnp.stack(
        [(x_index - k) % x_count * 2 + (core + other) % 2 for other in (0, 1) for k in range(x_count)]
    )

    def words_of(targets):
        targets = targets.reshape(CHAIN, mp_count, 1, share_rows)[:, mp_order]
        targets = jnp.broadcast_to(targets, (CHAIN, mp_count, models, share_rows))
        return targets.reshape(CHAIN, 2, x_count, each)

    tiles = 2 if part % 256 == 0 else 1

    def place_head():
        pieces, firsts = [], []
        for cut, others in enumerate(besides_head):
            pieces += [came_head[cut]] + others
            for source in [seq_index] + [from_partner(side, block) for side, block in partners]:
                first_of_chain = source - place_of(source) * SIDE
                firsts += [
                    (first_of_chain + k * SIDE) * head_rows + cut * cut_rows for k in range(CHAIN)
                ]
        return pl.pallas_call(
            functools.partial(place_kernel, len(pieces)),
            in_specs=[pl.BlockSpec(memory_space=pltpu.SMEM)]
            + [pl.BlockSpec(memory_space=pl.ANY)] * len(pieces),
            out_specs=pl.BlockSpec(memory_space=pltpu.VMEM),
            out_shape=jax.ShapeDtypeStruct((seq_count * head_rows, part), vocab_head_weight.dtype),
            scratch_shapes=[pltpu.SemaphoreType.DMA((len(pieces) * CHAIN,))],
            compiler_params=pltpu.CompilerParams(vmem_limit_bytes=16 * 2**20),
            cost_estimate=cost(0, 4 * seq_count * head_rows * part),
            name="place_head_rows",
        )(jnp.stack(firsts).astype(jnp.int32), *pieces)

    def head_stats(head_part, rows, words):
        count = len(rows)
        words = words.reshape(count * each, 1)
        stats_shape = jax.ShapeDtypeStruct((8, count * each), jnp.float32)
        return pl.pallas_call(
            functools.partial(head_kernel, count),
            in_specs=[pl.BlockSpec(memory_space=pltpu.SMEM)]
            + [pl.BlockSpec(memory_space=pltpu.VMEM)] * count
            + [pl.BlockSpec(memory_space=pl.ANY), pl.BlockSpec(memory_space=pltpu.VMEM)],
            out_specs=pl.BlockSpec(memory_space=pltpu.VMEM),
            out_shape=stats_shape,
            scratch_shapes=[
                pltpu.VMEM((tiles, width, part // tiles), jnp.bfloat16),
                pltpu.VMEM((count * each, part), jnp.float32),
                pltpu.SemaphoreType.DMA((tiles,)),
            ],
            compiler_params=pltpu.CompilerParams(vmem_limit_bytes=56 * 2**20),
            cost_estimate=cost(
                2 * count * each * width * part,
                2 * (count * each + part) * width,
                count * each * part,
            ),
            name="head_stats",
        )(limit, *rows, head_part, words).reshape(8, count, models, share_rows)

    def both_cores(values):
        return values + [other_core(value) for value in values]

    def crossed(rows):
        return [along_x(rows, by) for by in range(1, x_count)]

    blocks_of = [normed_own]
    nears = [crossed(normed_own)]
    words = words_of(words_and_valid[:, 0])
    at_end = (place == 0) | (place == CHAIN - 1)
    for step in range(1, CHAIN):
        if step == 1:
            moved = [turn(normed_own, 1), between(normed_own, [(1, 2), (2, 1)])]
        elif step == 2:
            moved = [between(inner, [(1, 0), (2, 3)]), between(blocks_of[1], [(1, 2), (2, 1)])]
        else:
            moved = [between(passed, [(1, 0), (2, 3)])]
        count = len(nears[-1])
        extra = []
        if step == 1:
            extra = besides_head[0]
        elif step == CHAIN - 2:
            extra = besides_head[-1]
        elif step == CHAIN - 1:
            head_part = place_head()
            rows = both_cores([blocks_of[0]] + nears[0])
            extra = [head_stats(head_part, rows, words[0])]
        came = tied(*nears[-1], *extra, *moved)
        nears[-1], extra, moved = came[:count], came[count : -len(moved)], came[-len(moved) :]
        if step == 1:
            besides_head[0] = extra
        elif step == CHAIN - 2:
            besides_head[-1] = extra
        elif step == CHAIN - 1:
            early = extra[0]
        if step == 1:
            block, inner = moved
        elif step == 2:
            passed = moved[1]
            block = jnp.where(at_end, moved[0], passed)
        else:
            block = jnp.where(at_end, moved[0], inner)
        blocks_of.append(block)
        nears.append(crossed(block))

    last = CHAIN - 1
    rows = [both_cores([blocks_of[k]] + nears[k]) for k in range(1, last)]
    middle = head_stats(
        head_part,
        [value for values in rows for value in values] + both_cores([blocks_of[last]]),
        jnp.concatenate([words[1:last].reshape(-1, each), words[last, :, 0]]),
    )
    def blocks(stats):
        return stats[:3].reshape(3, -1, 2, x_count, models, share_rows)

    *nears[last], middle, early = tied(*nears[last], middle, early)
    rest = head_stats(head_part, both_cores(nears[last]), words[last, :, 1:])
    whole_blocks = (last - 1) * mp_count
    own_side = middle[:3, whole_blocks:].reshape(3, 1, 2, 1, models, share_rows)
    other_side = rest[:3].reshape(3, 1, 2, x_count - 1, models, share_rows)
    stats = jnp.concatenate(
        [
            blocks(early),
            blocks(middle[:, :whole_blocks]),
            jnp.concatenate([own_side, other_side], axis=3),
        ],
        axis=1,
    )

    def merged(several):
        top = functools.reduce(jnp.maximum, [stats[0] for stats in several])
        total = sum(stats[1] * jnp.exp(stats[0] - top) for stats in several)
        return jnp.stack([top, total, sum(stats[2] for stats in several)])

    several = [stats]
    for by in range(1, CHAIN):
        came = turn(stats, by)
        several.append(jnp.stack([came[:, k ^ by] for k in range(CHAIN)], axis=1))
    stats = merged(several)
    several = [stats, other_core(stats)[:, :, ::-1]]
    for by in range(1, x_count):
        several.append(jnp.roll(along_x(stats, by), by, axis=3))
        several.append(jnp.roll(across(stats, by)[:, :, ::-1], by, axis=3))
    stats = merged(several)
    logprob = stats[2] - stats[0] - jnp.log(stats[1])
    delta = (logprob[:, :, :, 0] - logprob[:, :, :, 1]).reshape(CHAIN, mp_count, share_rows)
    in_order = mp_order[None, :] == quarter[:, None]
    delta = jnp.sum(jnp.where(in_order[None, :, :, None], delta[:, None], 0.0), axis=2)
    delta = delta.reshape(CHAIN, tok_rows) * words_and_valid[:, 1].astype(jnp.float32)
    token_delta = delta[0]
    first_rows = jnp.stack([turned(seq_index, k) for k in range(CHAIN)]) * tok_rows
    since = (first_rows[:, None] + offsets[None, :])[:, :, None] - starts
    member = ((since >= 0) & (since < lengths)).astype(jnp.float32)
    roll_sums = jnp.dot(
        delta.reshape(-1), member.reshape(-1, roll_count), precision=highest
    )
    roll_sums = roll_sums + sum(beside(roll_sums))
    owner_sums = jnp.where(owners == seq_index, roll_sums / lengths.astype(jnp.float32), 0.0)
    return (owner_sums[None, :], token_delta)


def solution(mesh):
    placed = (
        P("seq"),
        P("seq"),
        P(),
        P(),
        P(),
        P(None, "seq", "mp"),
        P(None, "seq", "mp"),
        P(None, "seq", None),
        P(None, "seq", None),
        P(None, "seq", "mp"),
        P(None, "mp"),
        P(None, "mp"),
        P(None, "seq", "mp", None, None),
        P("mp", None),
        P("mp", None),
        P(),
        P("seq", None, None),
        P(),
        P("seq", "mp"),
    )
    return jax.shard_map(
        shards, mesh=mesh, in_specs=placed, out_specs=(P("seq", None), P("seq")), check_vma=False
    )
```
